512 devices in a mesh: ctx: 64 (over y, z), exp: 8 (over x, core).
Axes of the slice: x: 4, y: 4, z: 16, core: 2. Of those that a mesh axis runs over, the one named last changes fastest.
Arguments:
- patches: bfloat16 [8, 32768, 1280], P('exp', 'ctx'), may hold values from -36 to 300
- router: bfloat16 [1280, 32], replicated, may hold values from -1 to 1.1
- w_in: bfloat16 [32, 1280, 5120], P('exp', None, 'ctx'), may hold values from -0.15625 to 0.15625
- w_out: bfloat16 [32, 5120, 1280], P('exp', 'ctx'), may hold values from -0.078125 to 0.078125
Outputs:
- mixed: bfloat16 [8, 32768, 1280], P('exp', 'ctx')
The draws below stay inside these ranges and needn't reach their ends.
All inputs are finite; a program needn't handle non-finite values.
Results may differ from the reference program's by a relative error of at most 0.012.
Values may be sent and summed in bfloat16 or wider, within the bound.
No kernel may reach another device: no remote copies, remote signals or barrier semaphores. Data moves between devices by JAX's collectives and lax.ppermute only.
A program may use at most 64 MiB of HBM per device.

```python
import jax
import jax.numpy as jnp
from jax import lax

D = 1280
FF = 5120
EXPERTS = 32
SLIDES = 8
SLIDE_PATCHES = 32768


def draw_patches(key, part):
    key = jax.random.fold_in(key, 11)
    first, second = jax.random.split(key, 2)
    base = jnp.clip(jax.random.normal(first, (SLIDES, SLIDE_PATCHES, D), jnp.float32), -6.0, 6.0)
    rows = jnp.arange(SLIDE_PATCHES, dtype=jnp.float32)[None, :, None]
    spread = jnp.exp(jax.random.uniform(second, (SLIDES, SLIDE_PATCHES, 1), jnp.float32, jnp.log(0.5), jnp.log(2.0)))
    values = base * (1.0 + 2.0 * rows / SLIDE_PATCHES) * spread
    return values.astype(jnp.bfloat16)


def draw_router(key, part):
    key = jax.random.fold_in(key, 12)
    first = jax.random.fold_in(key, 0)
    values = jnp.clip(jax.random.normal(first, (D, EXPERTS), jnp.float32), -6.0, 6.0) / jnp.sqrt(jnp.float32(D))
    return values.astype(jnp.bfloat16)


def steps_of(stream_key, shape, shards, low, top_value):
    gain = 1.0
    for position, parts in shards:
        heights = jax.random.uniform(jax.random.fold_in(jax.random.fold_in(stream_key, 6), position), (parts,), jnp.float32, low / len(shards), top_value / len(shards))
        gain = gain * jnp.repeat(jnp.exp(heights), shape[position] // parts).reshape((-1,) + (1,) * (len(shape) - 1 - position))
    return gain


def noise(key, extent, deviation, most, cuts=(), kind=jnp.bfloat16):
    array = jax.random.normal(key, extent, jnp.float32) * deviation
    if len(cuts) > 0:
        array = steps_of(key, extent, cuts, -0.22, 0.18) * array
    return jnp.clip(array, min=-most, max=most).astype(kind)


def setup_inputs(seed: int = 0) -> dict:
    key_list = jax.random.split(jax.random.key(seed), 5)
    patches = draw_patches(jax.random.fold_in(key_list[4], 71), 0)
    router = draw_router(jax.random.fold_in(key_list[4], 71), 0)
    w_in = noise(key_list[2], (EXPERTS, D, FF), D ** -0.5, 0.15625, ((0, 8), (2, 64)))
    w_out = noise(key_list[3], (EXPERTS, FF, D), FF ** -0.5, 0.078125, ((0, 8), (1, 64)))
    return dict(patches=patches, router=router, w_in=w_in, w_out=w_out)


def reference(patches, router, w_in, w_out):
    def slide_in(rows):
        logits = jnp.dot(rows, router, preferred_element_type=jnp.float32)
        slot_max = jnp.max(logits, axis=0)
        weights = jnp.exp(logits - slot_max[None, :])
        slot_total = jnp.sum(weights, axis=0)
        dispatch = weights.astype(jnp.bfloat16)
        slot_sum = jnp.dot(dispatch.T, rows, preferred_element_type=jnp.float32)
        return (slot_sum / slot_total[:, None]).astype(jnp.bfloat16)

    slot_in = lax.map(slide_in, patches)

    def expert(items):
        inputs, first, second = items
        hidden = jax.nn.gelu(jnp.dot(inputs, first, preferred_element_type=jnp.float32)).astype(jnp.bfloat16)
        return jnp.dot(hidden, second, preferred_element_type=jnp.float32).astype(jnp.bfloat16)

    slot_out = lax.map(expert, (jnp.transpose(slot_in, (1, 0, 2)), w_in, w_out))
    slot_out = jnp.transpose(slot_out, (1, 0, 2))

    def slide_out(items):
        rows, outputs = items
        logits = jnp.dot(rows, router, preferred_element_type=jnp.float32)
        row_max = jnp.max(logits, axis=1, keepdims=True)
        combine = jnp.exp(logits - row_max)
        row_total = jnp.sum(combine, axis=1, keepdims=True)
        mixed = jnp.dot(combine.astype(jnp.bfloat16), outputs, preferred_element_type=jnp.float32) / row_total
        return mixed.astype(jnp.bfloat16)

    return lax.map(slide_out, (patches, slot_out))
```

```python
import jax
import jax.numpy as jnp
from jax import lax
from jax.sharding import Mesh, PartitionSpec as P

Y, Z, X, C = 4, 16, 4, 2
ZL = 1
ZH = Z // ZL
LANES = 384
BF = jnp.bfloat16
F32 = jnp.float32
NEAR = ("y", "zl", "x", "c")


def exact_parts(v):
    high = lax.reduce_precision(v, 8, 7)
    rest = v - high
    mid = lax.reduce_precision(rest, 8, 7)
    low = rest - mid
    return jnp.stack([high, mid, low], axis=-1).astype(BF)


def packed(mean, lse):
    pad = LANES - mean.shape[-1] - 3
    tail = jnp.pad(exact_parts(lse), [(0, 0)] * lse.ndim + [(0, pad)])
    tail = jnp.broadcast_to(tail, mean.shape[:-1] + (tail.shape[-1],))
    return jnp.concatenate([mean.astype(BF), tail], axis=-1)


def merged(pieces, width):
    mean = pieces[..., :width].astype(F32)
    lse = jnp.sum(pieces[..., width : width + 3].astype(F32), axis=-1)
    top = jnp.max(lse, axis=0)
    weight = jnp.exp(lse - top)
    total = jnp.sum(weight, axis=0)
    mean = jnp.sum(mean * weight[..., None], axis=0) / total[..., None]
    return mean, top + jnp.log(total)


def spread(block, axes, count):
    copies = jnp.broadcast_to(block[None], (count,) + block.shape)
    return lax.all_to_all(copies, axes, 0, 0, tiled=True)


def on_device(patches, router, w_in, w_out):
    rows = patches[0]
    own = w_in.shape[0]
    slots = router.shape[1]
    groups = slots // own
    depth = rows.shape[1]
    width = depth // Y
    part = own // ZL

    logits = jnp.dot(rows, router, preferred_element_type=F32)
    local_max = jnp.max(logits, axis=0)
    weights = jnp.exp(logits - local_max[None, :])
    local_total = jnp.sum(weights, axis=0)
    local_sum = lax.dot_general(
        weights.astype(BF), rows, (((0,), (0,)), ((), ())), preferred_element_type=F32
    )
    mean = local_sum / local_total[:, None]
    lse = local_max + jnp.log(local_total)

    mean = mean.reshape(groups, ZL, part, Y, width).transpose(3, 1, 0, 2, 4)
    lse = lse.reshape(1, groups, ZL, part).transpose(0, 2, 1, 3)
    pieces = packed(mean, lse).reshape(Y * ZL * groups, part, LANES)
    got = lax.all_to_all(pieces, NEAR, 0, 0, tiled=True)
    mean, lse = merged(got.reshape(Y * ZL, groups * part, LANES), width)
    got = spread(packed(mean, lse), "zh", ZH)
    mean, _ = merged(got, width)
    got = spread(mean.astype(BF), ("y", "zl"), Y * ZL)
    slot_in = got.reshape(Y, ZL, groups, part, width).transpose(2, 1, 3, 0, 4).reshape(groups, own, depth)

    hidden = jax.nn.gelu(jnp.einsum("bed,edf->bef", slot_in, w_in, preferred_element_type=F32)).astype(BF)
    partial_out = jnp.einsum("bef,efd->bed", hidden, w_out, preferred_element_type=F32).astype(BF)

    pieces = partial_out.reshape(groups, ZL, part, Y, width).transpose(3, 1, 0, 2, 4)
    got = lax.all_to_all(pieces.reshape(Y * ZL * groups, part, width), NEAR, 0, 0, tiled=True)
    total = jnp.sum(got.reshape(Y * ZL, groups * part, width).astype(F32), axis=0).astype(BF)
    got = spread(total, "zh", ZH)
    total = jnp.sum(got.astype(F32), axis=0).astype(BF)
    got = spread(total, ("y", "zl"), Y * ZL)
    slot_out = got.reshape(Y, ZL, groups, part, width).transpose(2, 1, 3, 0, 4).reshape(slots, depth)

    row_max = jnp.max(logits, axis=1, keepdims=True)
    combine = jnp.exp(logits - row_max)
    row_total = jnp.sum(combine, axis=1, keepdims=True)
    mixed = jnp.dot(combine.astype(BF), slot_out, preferred_element_type=F32)
    return (mixed / row_total).astype(BF)[None]


def solution(mesh):
    fine = Mesh(mesh.devices.reshape(Y, ZH, ZL, X, C), ("y", "zh", "zl", "x", "c"))
    ctx, exp = ("y", "zh", "zl"), ("x", "c")
    placed = (P(exp, ctx, None), P(), P(exp, None, ctx), P(exp, ctx, None))
    return jax.shard_map(
        on_device, mesh=fine, in_specs=placed, out_specs=P(exp, ctx, None), check_vma=False
    )
```

```python
import jax
import jax.numpy as jnp
from jax import lax
from jax.sharding import Mesh, PartitionSpec as P

Y, Z, X, C = 4, 16, 4, 2
ZL = 2
ZH = Z // ZL
LANES = 384
BF = jnp.bfloat16
F32 = jnp.float32
NEAR = ("y", "zl", "x", "c")


def exact_parts(v):
    high = lax.reduce_precision(v, 8, 7)
    rest = v - high
    mid = lax.reduce_precision(rest, 8, 7)
    low = rest - mid
    return jnp.stack([high, mid, low], axis=-1).astype(BF)


def packed(mean, lse):
    pad = LANES - mean.shape[-1] - 3
    tail = jnp.pad(exact_parts(lse), [(0, 0)] * lse.ndim + [(0, pad)])
    tail = jnp.broadcast_to(tail, mean.shape[:-1] + (tail.shape[-1],))
    return jnp.concatenate([mean.astype(BF), tail], axis=-1)


def merged(pieces, width):
    mean = pieces[..., :width].astype(F32)
    lse = jnp.sum(pieces[..., width : width + 3].astype(F32), axis=-1)
    top = jnp.max(lse, axis=0)
    weight = jnp.exp(lse - top)
    total = jnp.sum(weight, axis=0)
    mean = jnp.sum(mean * weight[..., None], axis=0) / total[..., None]
    return mean, top + jnp.log(total)


def spread(block, axes, count):
    copies = jnp.broadcast_to(block[None], (count,) + block.shape)
    return lax.all_to_all(copies, axes, 0, 0, tiled=True)


def on_device(patches, router, w_in, w_out):
    rows = patches[0]
    own = w_in.shape[0]
    slots = router.shape[1]
    groups = slots // own
    depth = rows.shape[1]
    width = depth // Y
    part = own // ZL

    logits = jnp.dot(rows, router, preferred_element_type=F32)
    local_max = jnp.max(logits, axis=0)
    weights = jnp.exp(logits - local_max[None, :])
    local_total = jnp.sum(weights, axis=0)
    local_sum = lax.dot_general(
        weights.astype(BF), rows, (((0,), (0,)), ((), ())), preferred_element_type=F32
    )
    mean = local_sum / local_total[:, None]
    lse = local_max + jnp.log(local_total)

    mean = mean.reshape(groups, ZL, part, Y, width).transpose(3, 1, 0, 2, 4)
    lse = lse.reshape(1, groups, ZL, part).transpose(0, 2, 1, 3)
    pieces = packed(mean, lse).reshape(Y * ZL * groups, part, LANES)
    got = lax.all_to_all(pieces, NEAR, 0, 0, tiled=True)
    mean, lse = merged(got.reshape(Y * ZL, groups * part, LANES), width)
    got = spread(packed(mean, lse), "zh", ZH)
    mean, _ = merged(got, width)
    got = spread(mean.astype(BF), ("y", "zl"), Y * ZL)
    slot_in = got.reshape(Y, ZL, groups, part, width).transpose(2, 1, 3, 0, 4).reshape(groups, own, depth)

    hidden = jax.nn.gelu(jnp.einsum("bed,edf->bef", slot_in, w_in, preferred_element_type=F32)).astype(BF)
    partial_out = jnp.einsum("bef,efd->bed", hidden, w_out, preferred_element_type=F32).astype(BF)

    pieces = partial_out.reshape(groups, ZL, part, Y, width).transpose(3, 1, 0, 2, 4)
    got = lax.all_to_all(pieces.reshape(Y * ZL * groups, part, width), NEAR, 0, 0, tiled=True)
    total = jnp.sum(got.reshape(Y * ZL, groups * part, width).astype(F32), axis=0).astype(BF)
    got = spread(total, "zh", ZH)
    total = jnp.sum(got.astype(F32), axis=0).astype(BF)
    got = spread(total, ("y", "zl"), Y * ZL)
    slot_out = got.reshape(Y, ZL, groups, part, width).transpose(2, 1, 3, 0, 4).reshape(slots, depth)

    row_max = jnp.max(logits, axis=1, keepdims=True)
    combine = jnp.exp(logits - row_max)
    row_total = jnp.sum(combine, axis=1, keepdims=True)
    mixed = jnp.dot(combine.astype(BF), slot_out, preferred_element_type=F32)
    return (mixed / row_total).astype(BF)[None]


def solution(mesh):
    fine = Mesh(mesh.devices.reshape(Y, ZH, ZL, X, C), ("y", "zh", "zl", "x", "c"))
    ctx, exp = ("y", "zh", "zl"), ("x", "c")
    placed = (P(exp, ctx, None), P(), P(exp, None, ctx), P(exp, ctx, None))
    return jax.shard_map(
        on_device, mesh=fine, in_specs=placed, out_specs=P(exp, ctx, None), check_vma=False
    )
```

```python
import jax
import jax.numpy as jnp
from jax import lax
from jax.sharding import Mesh, PartitionSpec as P

Y, Z, X, C = 4, 16, 4, 2
ZL = 2
ZH = Z // ZL
LANES = 768
BF = jnp.bfloat16
F32 = jnp.float32
NEAR = ("y", "zl", "x", "c")


def exact_parts(v):
    high = lax.reduce_precision(v, 8, 7)
    rest = v - high
    mid = lax.reduce_precision(rest, 8, 7)
    low = rest - mid
    return jnp.stack([high, mid, low], axis=-1).astype(BF)


def packed(mean, lse):
    pad = LANES - mean.shape[-1] - 3
    tail = jnp.pad(exact_parts(lse), [(0, 0)] * lse.ndim + [(0, pad)])
    tail = jnp.broadcast_to(tail, mean.shape[:-1] + (tail.shape[-1],))
    return jnp.concatenate([mean.astype(BF), tail], axis=-1)


def merged(pieces, width):
    mean = pieces[..., :width].astype(F32)
    lse = jnp.sum(pieces[..., width : width + 3].astype(F32), axis=-1)
    top = jnp.max(lse, axis=0)
    weight = jnp.exp(lse - top)
    total = jnp.sum(weight, axis=0)
    mean = jnp.sum(mean * weight[..., None], axis=0) / total[..., None]
    return mean, top + jnp.log(total)


def spread(block, axes, count):
    copies = jnp.broadcast_to(block[None], (count,) + block.shape)
    return lax.all_to_all(copies, axes, 0, 0, tiled=True)


def on_device(patches, router, w_in, w_out):
    rows = patches[0]
    own = w_in.shape[0]
    slots = router.shape[1]
    groups = slots // own
    depth = rows.shape[1]
    width = depth // ZL

    logits = jnp.dot(rows, router, preferred_element_type=F32)
    local_max = jnp.max(logits, axis=0)
    weights = jnp.exp(logits - local_max[None, :])
    local_total = jnp.sum(weights, axis=0)
    local_sum = lax.dot_general(
        weights.astype(BF), rows, (((0,), (0,)), ((), ())), preferred_element_type=F32
    )
    mean = local_sum / local_total[:, None]
    lse = local_max + jnp.log(local_total)

    mean = mean.reshape(groups, Y, ZL, width).transpose(1, 2, 0, 3)
    lse = jnp.broadcast_to(lse.reshape(groups, Y).T[:, None], (Y, ZL, groups))
    pieces = packed(mean, lse).reshape(Y * ZL * groups, LANES)
    got = lax.all_to_all(pieces, NEAR, 0, 0, tiled=True)
    mean, lse = merged(got.reshape(Y * ZL, groups, LANES), width)
    got = spread(packed(mean, lse), "zh", ZH)
    mean, _ = merged(got, width)
    got = spread(mean.astype(BF), ("y", "zl"), Y * ZL)
    slot_in = got.reshape(Y, ZL, groups, width).transpose(2, 0, 1, 3).reshape(groups, own, depth)

    hidden = jax.nn.gelu(jnp.einsum("bed,edf->bef", slot_in, w_in, preferred_element_type=F32)).astype(BF)
    partial_out = jnp.einsum("bef,efd->bed", hidden, w_out, preferred_element_type=F32).astype(BF)

    pieces = partial_out.reshape(groups, Y, ZL, width).transpose(1, 2, 0, 3)
    got = lax.all_to_all(pieces.reshape(Y * ZL * groups, width), NEAR, 0, 0, tiled=True)
    total = jnp.sum(got.reshape(Y * ZL, groups, width).astype(F32), axis=0).astype(BF)
    got = spread(total, "zh", ZH)
    total = jnp.sum(got.astype(F32), axis=0).astype(BF)
    got = spread(total, ("y", "zl"), Y * ZL)
    slot_out = got.reshape(Y, ZL, groups, width).transpose(2, 0, 1, 3).reshape(slots, depth)

    row_max = jnp.max(logits, axis=1, keepdims=True)
    combine = jnp.exp(logits - row_max)
    row_total = jnp.sum(combine, axis=1, keepdims=True)
    mixed = jnp.dot(combine.astype(BF), slot_out, preferred_element_type=F32)
    return (mixed / row_total).astype(BF)[None]


def solution(mesh):
    fine = Mesh(mesh.devices.reshape(Y, ZH, ZL, X, C), ("y", "zh", "zl", "x", "c"))
    ctx, exp = ("y", "zh", "zl"), ("x", "c")
    placed = (P(exp, ctx, None), P(), P(exp, None, ctx), P(exp, ctx, None))
    return jax.shard_map(
        on_device, mesh=fine, in_specs=placed, out_specs=P(exp, ctx, None), check_vma=False
    )
```

```python
import functools

import jax
import jax.numpy as jnp
from jax import lax
from jax.experimental import pallas as pl
from jax.experimental.pallas import tpu as pltpu
from jax.sharding import Mesh, PartitionSpec as P

Y, Z, X, C = 4, 16, 4, 2
ZL = 2
ZH = Z // ZL
EXTRA = 128
BF = jnp.bfloat16
F32 = jnp.float32
NEAR = ("y", "zl", "x", "c")


def slot_kernel(groups, rows_hbm, router_hbm, pieces_ref, combine_ref, rows, router_in, sems):
    count, depth = rows_hbm.shape
    width = depth // ZL
    first = pltpu.make_async_copy(router_hbm, router_in, sems.at[0])
    second = pltpu.make_async_copy(rows_hbm, rows, sems.at[1])
    first.start()
    second.start()
    first.wait()

    slots = router_in.shape[0]
    row = lax.broadcasted_iota(jnp.int32, (slots, slots), 0)
    column = lax.broadcasted_iota(jnp.int32, (slots, slots), 1)
    chosen = (column == (row % groups) * Y + row // groups).astype(F32).astype(BF)
    router = jnp.dot(chosen, router_in[...], preferred_element_type=F32).astype(BF)
    second.wait()
    values = lax.dot_general(router, rows[...], (((1,), (1,)), ((), ())), preferred_element_type=F32)
    top = jnp.max(values, axis=1, keepdims=True)
    weights = jnp.exp(values - top)
    total = jnp.sum(weights, axis=1, keepdims=True)
    summed = jnp.dot(weights.astype(BF), rows[...], preferred_element_type=F32)
    mean = summed / total
    lse = top + jnp.log(total)
    high = lse.astype(BF).astype(F32)
    mid = (lse - high).astype(BF).astype(F32)
    low = lse - high - mid
    lane = lax.broadcasted_iota(jnp.int32, (slots, EXTRA), 1)
    tail = jnp.where(lane == 0, high, jnp.where(lane == 1, mid, jnp.where(lane == 2, low, 0.0)))
    size = groups * ZL
    for y in range(Y):
        block = mean[y * groups : (y + 1) * groups]
        halves = [block[:, z * width : (z + 1) * width] for z in range(ZL)]
        pieces_ref[y * size : (y + 1) * size, :width] = jnp.concatenate(halves, axis=0).astype(BF)
        end = tail[y * groups : (y + 1) * groups]
        pieces_ref[y * size : (y + 1) * size, width:] = jnp.concatenate([end] * ZL, axis=0).astype(BF)

    combine = jnp.exp(values - jnp.max(values, axis=0, keepdims=True))
    combine_ref[...] = (combine / jnp.sum(combine, axis=0, keepdims=True)).astype(BF)


def in_hbm(array):
    return pltpu.with_memory_space_constraint(array, pltpu.HBM)


def slot_sums(rows, router, groups):
    count, depth = rows.shape
    slots = router.shape[1]
    width = depth // ZL
    return pl.pallas_call(
        functools.partial(slot_kernel, groups),
        out_shape=(
            jax.ShapeDtypeStruct((slots * ZL, width + EXTRA), BF),
            jax.ShapeDtypeStruct((slots, count), BF),
        ),
        in_specs=[pl.BlockSpec(memory_space=pltpu.HBM), pl.BlockSpec(memory_space=pltpu.HBM)],
        out_specs=(pl.BlockSpec(memory_space=pltpu.VMEM), pl.BlockSpec(memory_space=pltpu.VMEM)),
        scratch_shapes=[
            pltpu.VMEM((count, depth), BF),
            pltpu.VMEM((slots, depth), BF),
            pltpu.SemaphoreType.DMA((2,)),
        ],
        compiler_params=pltpu.CompilerParams(vmem_limit_bytes=32 * 1024 * 1024),
        name="slot_sums",
    )(in_hbm(rows), in_hbm(router.T))


def exact_parts(v):
    high = lax.reduce_precision(v, 8, 7)
    rest = v - high
    mid = lax.reduce_precision(rest, 8, 7)
    low = rest - mid
    return jnp.stack([high, mid, low], axis=-1).astype(BF)


def packed(mean, lse):
    tail = jnp.pad(exact_parts(lse), [(0, 0)] * lse.ndim + [(0, EXTRA - 3)])
    return jnp.concatenate([mean.astype(BF), tail], axis=-1)


def merged(pieces, width):
    mean = pieces[..., :width].astype(F32)
    lse = jnp.sum(pieces[..., width : width + 3].astype(F32), axis=-1)
    top = jnp.max(lse, axis=0)
    weight = jnp.exp(lse - top)
    total = jnp.sum(weight, axis=0)
    mean = jnp.sum(mean * weight[..., None], axis=0) / total[..., None]
    return mean, top + jnp.log(total)


def scatter(pieces):
    count, width = pieces.shape
    got = lax.all_to_all(pieces.reshape(count, 2, width // 2), NEAR, 0, 0, tiled=True)
    return got.reshape(Y * ZL, count // (Y * ZL), width)


def spread(block, axes, count):
    copies = jnp.broadcast_to(block[None], (count,) + block.shape)
    return lax.all_to_all(copies, axes, 0, 0, tiled=True)


def on_device(patches, router, w_in, w_out):
    own = w_in.shape[0]
    slots = router.shape[1]
    groups = slots // own
    depth = patches.shape[2]
    width = depth // ZL

    pieces, combine = slot_sums(patches[0], router, groups)
    mean, lse = merged(scatter(pieces), width)
    got = spread(packed(mean, lse), "zh", ZH)
    mean, _ = merged(got, width)
    got = spread(mean.astype(BF), ("y", "zl"), Y * ZL)
    slot_in = got.reshape(Y, ZL, groups, width).transpose(2, 0, 1, 3).reshape(groups, own, depth)

    hidden = jax.nn.gelu(jnp.einsum("bed,edf->bef", slot_in, w_in, preferred_element_type=F32)).astype(BF)
    partial_out = jnp.einsum("bef,efd->bed", hidden, w_out, preferred_element_type=F32).astype(BF)

    pieces = partial_out.reshape(groups, Y, ZL, width).transpose(1, 2, 0, 3).reshape(Y * ZL * groups, width)
    total = jnp.sum(scatter(pieces).astype(F32), axis=0).astype(BF)
    got = spread(total, "zh", ZH)
    total = jnp.sum(got.astype(F32), axis=0).astype(BF)
    got = spread(total, ("y", "zl"), Y * ZL)
    slot_out = got.reshape(Y, ZL, groups, width).transpose(0, 2, 1, 3).reshape(slots, depth)

    mixed = lax.dot_general(combine, slot_out, (((0,), (0,)), ((), ())), preferred_element_type=F32)
    return mixed.astype(BF)[None]


def solution(mesh):
    fine = Mesh(mesh.devices.reshape(Y, ZH, ZL, X, C), ("y", "zh", "zl", "x", "c"))
    ctx, exp = ("y", "zh", "zl"), ("x", "c")
    placed = (P(exp, ctx, None), P(), P(exp, None, ctx), P(exp, ctx, None))
    return jax.shard_map(
        on_device, mesh=fine, in_specs=placed, out_specs=P(exp, ctx, None), check_vma=False
    )
```

```python
import functools

import jax
import jax.numpy as jnp
from jax import lax
from jax.experimental import pallas as pl
from jax.experimental.pallas import tpu as pltpu
from jax.sharding import Mesh, PartitionSpec as P

Y, Z, X, C = 4, 16, 4, 2
ZL = 2
ZH = Z // ZL
EXTRA = 128
BF = jnp.bfloat16
F32 = jnp.float32
NEAR = ("y", "zl", "x", "c")


def slot_kernel(groups, rows_hbm, router_hbm, pieces_ref, combine_ref, rows, router_in, sems):
    count, depth = rows_hbm.shape
    width = depth // ZL
    first = pltpu.make_async_copy(router_hbm, router_in, sems.at[0])
    second = pltpu.make_async_copy(rows_hbm, rows, sems.at[1])
    first.start()
    second.start()
    first.wait()

    slots = router_in.shape[0]
    row = lax.broadcasted_iota(jnp.int32, (slots, slots), 0)
    column = lax.broadcasted_iota(jnp.int32, (slots, slots), 1)
    chosen = (column == (row % groups) * Y + row // groups).astype(F32).astype(BF)
    router = jnp.dot(chosen, router_in[...], preferred_element_type=F32).astype(BF)
    second.wait()
    values = lax.dot_general(router, rows[...], (((1,), (1,)), ((), ())), preferred_element_type=F32)
    top = jnp.max(values, axis=1, keepdims=True)
    weights = jnp.exp(values - top)
    total = jnp.sum(weights, axis=1, keepdims=True)
    summed = jnp.dot(weights.astype(BF), rows[...], preferred_element_type=F32)
    mean = summed / total
    lse = top + jnp.log(total)
    high = lse.astype(BF).astype(F32)
    mid = (lse - high).astype(BF).astype(F32)
    low = lse - high - mid
    lane = lax.broadcasted_iota(jnp.int32, (slots, EXTRA), 1)
    tail = jnp.where(lane == 0, high, jnp.where(lane == 1, mid, jnp.where(lane == 2, low, 0.0)))
    size = groups * ZL
    for y in range(Y):
        block = mean[y * groups : (y + 1) * groups]
        halves = [block[:, z * width : (z + 1) * width] for z in range(ZL)]
        pieces_ref[y * size : (y + 1) * size, :width] = jnp.concatenate(halves, axis=0).astype(BF)
        end = tail[y * groups : (y + 1) * groups]
        pieces_ref[y * size : (y + 1) * size, width:] = jnp.concatenate([end] * ZL, axis=0).astype(BF)

    combine = jnp.exp(values - jnp.max(values, axis=0, keepdims=True))
    combine_ref[...] = (combine / jnp.sum(combine, axis=0, keepdims=True)).astype(BF)


def in_hbm(array):
    return pltpu.with_memory_space_constraint(array, pltpu.HBM)


def slot_sums(rows, router, groups):
    count, depth = rows.shape
    slots = router.shape[1]
    width = depth // ZL
    return pl.pallas_call(
        functools.partial(slot_kernel, groups),
        out_shape=(
            jax.ShapeDtypeStruct((slots * ZL, width + EXTRA), BF),
            jax.ShapeDtypeStruct((slots, count), BF),
        ),
        in_specs=[pl.BlockSpec(memory_space=pltpu.HBM), pl.BlockSpec(memory_space=pltpu.HBM)],
        out_specs=(pl.BlockSpec(memory_space=pltpu.VMEM), pl.BlockSpec(memory_space=pltpu.VMEM)),
        scratch_shapes=[
            pltpu.VMEM((count, depth), BF),
            pltpu.VMEM((slots, depth), BF),
            pltpu.SemaphoreType.DMA((2,)),
        ],
        compiler_params=pltpu.CompilerParams(vmem_limit_bytes=32 * 1024 * 1024),
        name="slot_sums",
    )(in_hbm(rows), in_hbm(router.T))


def exact_parts(v):
    high = lax.reduce_precision(v, 8, 7)
    rest = v - high
    mid = lax.reduce_precision(rest, 8, 7)
    low = rest - mid
    return jnp.stack([high, mid, low], axis=-1).astype(BF)


def packed(mean, lse):
    tail = jnp.pad(exact_parts(lse), [(0, 0)] * lse.ndim + [(0, EXTRA - 3)])
    return jnp.concatenate([mean.astype(BF), tail], axis=-1)


def merged(pieces, width):
    mean = pieces[..., :width].astype(F32)
    lse = jnp.sum(pieces[..., width : width + 3].astype(F32), axis=-1)
    top = jnp.max(lse, axis=0)
    weight = jnp.exp(lse - top)
    total = jnp.sum(weight, axis=0)
    mean = jnp.sum(mean * weight[..., None], axis=0) / total[..., None]
    return mean, top + jnp.log(total)


def scatter(pieces):
    count, width = pieces.shape
    got = lax.all_to_all(pieces.reshape(count, 2, width // 2), NEAR, 0, 0, tiled=True)
    return got.reshape(Y * ZL, count // (Y * ZL), width)


def spread(block, axes, count, first=0):
    copies = jnp.broadcast_to(block[None], (count,) + block.shape)
    order = [[(first + i) % count for i in range(count)]] if first else None
    return lax.all_to_all(copies, axes, 0, 0, tiled=True, axis_index_groups=order)


def on_device(patches, router, w_in, w_out):
    own = w_in.shape[0]
    slots = router.shape[1]
    groups = slots // own
    depth = patches.shape[2]
    width = depth // ZL

    pieces, combine = slot_sums(patches[0], router, groups)
    mean, lse = merged(scatter(pieces), width)
    got = spread(packed(mean, lse), "zh", ZH, ZH // 2)
    mean, _ = merged(got, width)
    got = spread(mean.astype(BF), ("y", "zl"), Y * ZL)
    slot_in = got.reshape(Y, ZL, groups, width).transpose(2, 0, 1, 3).reshape(groups, own, depth)

    hidden = jax.nn.gelu(jnp.einsum("bed,edf->bef", slot_in, w_in, preferred_element_type=F32)).astype(BF)
    partial_out = jnp.einsum("bef,efd->bed", hidden, w_out, preferred_element_type=F32).astype(BF)

    pieces = partial_out.reshape(groups, Y, ZL, width).transpose(1, 2, 0, 3).reshape(Y * ZL * groups, width)
    total = jnp.sum(scatter(pieces).astype(F32), axis=0).astype(BF)
    got = spread(total, "zh", ZH)
    total = jnp.sum(got.astype(F32), axis=0).astype(BF)
    got = spread(total, ("y", "zl"), Y * ZL)
    slot_out = got.reshape(Y, ZL, groups, width).transpose(0, 2, 1, 3).reshape(slots, depth)

    mixed = lax.dot_general(combine, slot_out, (((0,), (0,)), ((), ())), preferred_element_type=F32)
    return mixed.astype(BF)[None]


def solution(mesh):
    fine = Mesh(mesh.devices.reshape(Y, ZH, ZL, X, C), ("y", "zh", "zl", "x", "c"))
    ctx, exp = ("y", "zh", "zl"), ("x", "c")
    placed = (P(exp, ctx, None), P(), P(exp, None, ctx), P(exp, ctx, None))
    return jax.shard_map(
        on_device, mesh=fine, in_specs=placed, out_specs=P(exp, ctx, None), check_vma=False
    )
```

```python
import functools

import jax
import jax.numpy as jnp
from jax import lax
from jax.experimental import pallas as pl
from jax.experimental.pallas import tpu as pltpu
from jax.sharding import Mesh, PartitionSpec as P

Y, Z, X, C = 4, 16, 4, 2
ZL = 2
ZH = Z // ZL
EXTRA = 128
BF = jnp.bfloat16
F32 = jnp.float32
NEAR = ("y", "zl", "x", "c")


def slot_kernel(groups, rows_hbm, router_hbm, pieces_ref, combine_ref, rows, router_in, sems):
    count, depth = rows_hbm.shape
    width = depth // ZL
    first = pltpu.make_async_copy(router_hbm, router_in, sems.at[0])
    second = pltpu.make_async_copy(rows_hbm, rows, sems.at[1])
    first.start()
    second.start()
    first.wait()

    slots = router_in.shape[0]
    row = lax.broadcasted_iota(jnp.int32, (slots, slots), 0)
    column = lax.broadcasted_iota(jnp.int32, (slots, slots), 1)
    chosen = (column == (row % groups) * Y + row // groups).astype(F32).astype(BF)
    router = jnp.dot(chosen, router_in[...], preferred_element_type=F32).astype(BF)
    second.wait()
    values = lax.dot_general(router, rows[...], (((1,), (1,)), ((), ())), preferred_element_type=F32)
    top = jnp.max(values, axis=1, keepdims=True)
    weights = jnp.exp(values - top)
    total = jnp.sum(weights, axis=1, keepdims=True)
    summed = jnp.dot(weights.astype(BF), rows[...], preferred_element_type=F32)
    mean = summed / total
    lse = top + jnp.log(total)
    high = lse.astype(BF).astype(F32)
    mid = (lse - high).astype(BF).astype(F32)
    low = lse - high - mid
    lane = lax.broadcasted_iota(jnp.int32, (slots, EXTRA), 1)
    tail = jnp.where(lane == 0, high, jnp.where(lane == 1, mid, jnp.where(lane == 2, low, 0.0)))
    size = groups * ZL
    for y in range(Y):
        block = mean[y * groups : (y + 1) * groups]
        halves = [block[:, z * width : (z + 1) * width] for z in range(ZL)]
        pieces_ref[y * size : (y + 1) * size, :width] = jnp.concatenate(halves, axis=0).astype(BF)
        end = tail[y * groups : (y + 1) * groups]
        pieces_ref[y * size : (y + 1) * size, width:] = jnp.concatenate([end] * ZL, axis=0).astype(BF)

    combine = jnp.exp(values - jnp.max(values, axis=0, keepdims=True))
    combine_ref[...] = (combine / jnp.sum(combine, axis=0, keepdims=True)).astype(BF)


def in_hbm(array):
    return pltpu.with_memory_space_constraint(array, pltpu.HBM)


def slot_sums(rows, router, groups):
    count, depth = rows.shape
    slots = router.shape[1]
    width = depth // ZL
    return pl.pallas_call(
        functools.partial(slot_kernel, groups),
        out_shape=(
            jax.ShapeDtypeStruct((slots * ZL, width + EXTRA), BF),
            jax.ShapeDtypeStruct((slots, count), BF),
        ),
        in_specs=[pl.BlockSpec(memory_space=pltpu.HBM), pl.BlockSpec(memory_space=pltpu.HBM)],
        out_specs=(pl.BlockSpec(memory_space=pltpu.VMEM), pl.BlockSpec(memory_space=pltpu.VMEM)),
        scratch_shapes=[
            pltpu.VMEM((count, depth), BF),
            pltpu.VMEM((slots, depth), BF),
            pltpu.SemaphoreType.DMA((2,)),
        ],
        compiler_params=pltpu.CompilerParams(vmem_limit_bytes=32 * 1024 * 1024),
        name="slot_sums",
    )(in_hbm(rows), in_hbm(router.T))


def exact_parts(v):
    high = lax.reduce_precision(v, 8, 7)
    rest = v - high
    mid = lax.reduce_precision(rest, 8, 7)
    low = rest - mid
    return jnp.stack([high, mid, low], axis=-1).astype(BF)


def packed(mean, lse):
    tail = jnp.pad(exact_parts(lse), [(0, 0)] * lse.ndim + [(0, EXTRA - 3)])
    return jnp.concatenate([mean.astype(BF), tail], axis=-1)


def merged(pieces, width):
    mean = pieces[..., :width].astype(F32)
    lse = jnp.sum(pieces[..., width : width + 3].astype(F32), axis=-1)
    top = jnp.max(lse, axis=0)
    weight = jnp.exp(lse - top)
    total = jnp.sum(weight, axis=0)
    mean = jnp.sum(mean * weight[..., None], axis=0) / total[..., None]
    return mean, top + jnp.log(total)


def scatter(pieces):
    count, width = pieces.shape
    got = lax.all_to_all(pieces.reshape(count, 2, width // 2), NEAR, 0, 0, tiled=True)
    return got.reshape(Y * ZL, count // (Y * ZL), width)


def spread(block, axes, count, first=0):
    copies = jnp.broadcast_to(block[None], (count,) + block.shape)
    order = [[(first + i) % count for i in range(count)]] if first else None
    return lax.all_to_all(copies, axes, 0, 0, tiled=True, axis_index_groups=order)


def on_device(patches, router, w_in, w_out):
    own = w_in.shape[0]
    slots = router.shape[1]
    groups = slots // own
    depth = patches.shape[2]
    width = depth // ZL

    pieces, combine = slot_sums(patches[0], router, groups)
    mean, lse = merged(scatter(pieces), width)
    got = spread(packed(mean, lse), "zh", ZH, ZH // 2)
    mean, _ = merged(got, width)
    got = spread(mean.astype(BF), ("y", "zl"), Y * ZL)
    slot_in = got.reshape(Y, ZL, groups, width).transpose(2, 0, 1, 3).reshape(groups, own, depth)

    hidden = jax.nn.gelu(jnp.einsum("bed,edf->bef", slot_in, w_in, preferred_element_type=F32)).astype(BF)
    partial_out = jnp.einsum("bef,efd->bed", hidden, w_out, preferred_element_type=F32).astype(BF)

    pieces = partial_out.reshape(groups, Y, ZL, width).transpose(1, 2, 0, 3).reshape(Y * ZL * groups, width)
    total = jnp.sum(scatter(pieces).astype(F32), axis=0).astype(BF)
    got = spread(total, "zh", ZH, ZH // 2)
    total = jnp.sum(got.astype(F32), axis=0).astype(BF)
    got = spread(total, ("y", "zl"), Y * ZL)
    slot_out = got.reshape(Y, ZL, groups, width).transpose(0, 2, 1, 3).reshape(slots, depth)

    mixed = lax.dot_general(combine, slot_out, (((0,), (0,)), ((), ())), preferred_element_type=F32)
    return mixed.astype(BF)[None]


def solution(mesh):
    fine = Mesh(mesh.devices.reshape(Y, ZH, ZL, X, C), ("y", "zh", "zl", "x", "c"))
    ctx, exp = ("y", "zh", "zl"), ("x", "c")
    placed = (P(exp, ctx, None), P(), P(exp, None, ctx), P(exp, ctx, None))
    return jax.shard_map(
        on_device, mesh=fine, in_specs=placed, out_specs=P(exp, ctx, None), check_vma=False
    )
```

```python
import functools

import jax
import jax.numpy as jnp
from jax import lax
from jax.experimental import pallas as pl
from jax.experimental.pallas import tpu as pltpu
from jax.sharding import Mesh, PartitionSpec as P

Y, Z, X, C = 4, 16, 4, 2
ZL = 2
ZH = Z // ZL
EXTRA = 128
BF = jnp.bfloat16
F32 = jnp.float32
NEAR = ("y", "zl", "x", "c")
Y0, X0, H0 = 2, 2, ZH // 2


def rolled(*dims):
    members = [0]
    for size, first in dims:
        members = [m * size + (first + i) % size for m in members for i in range(size)]
    return [members]


def slot_kernel(groups, rows_hbm, router_hbm, pieces_ref, combine_ref, rows, router_in, sems):
    count, depth = rows_hbm.shape
    width = depth // ZL
    first = pltpu.make_async_copy(router_hbm, router_in, sems.at[0])
    second = pltpu.make_async_copy(rows_hbm, rows, sems.at[1])
    first.start()
    second.start()
    first.wait()

    slots = router_in.shape[0]
    row = lax.broadcasted_iota(jnp.int32, (slots, slots), 0)
    column = lax.broadcasted_iota(jnp.int32, (slots, slots), 1)
    chosen = (column == ((row + X0 * C) % groups) * Y + (row // groups + Y0) % Y).astype(F32).astype(BF)
    router = jnp.dot(chosen, router_in[...], preferred_element_type=F32).astype(BF)
    second.wait()
    values = lax.dot_general(router, rows[...], (((1,), (1,)), ((), ())), preferred_element_type=F32)
    top = jnp.max(values, axis=1, keepdims=True)
    weights = jnp.exp(values - top)
    total = jnp.sum(weights, axis=1, keepdims=True)
    summed = jnp.dot(weights.astype(BF), rows[...], preferred_element_type=F32)
    mean = summed / total
    lse = top + jnp.log(total)
    high = lse.astype(BF).astype(F32)
    mid = (lse - high).astype(BF).astype(F32)
    low = lse - high - mid
    lane = lax.broadcasted_iota(jnp.int32, (slots, EXTRA), 1)
    tail = jnp.where(lane == 0, high, jnp.where(lane == 1, mid, jnp.where(lane == 2, low, 0.0)))
    size = groups * ZL
    for y in range(Y):
        block = mean[y * groups : (y + 1) * groups]
        halves = [block[:, z * width : (z + 1) * width] for z in range(ZL)]
        pieces_ref[y * size : (y + 1) * size, :width] = jnp.concatenate(halves, axis=0).astype(BF)
        end = tail[y * groups : (y + 1) * groups]
        pieces_ref[y * size : (y + 1) * size, width:] = jnp.concatenate([end] * ZL, axis=0).astype(BF)

    combine = jnp.exp(values - jnp.max(values, axis=0, keepdims=True))
    combine_ref[...] = (combine / jnp.sum(combine, axis=0, keepdims=True)).astype(BF)


def in_hbm(array):
    return pltpu.with_memory_space_constraint(array, pltpu.HBM)


def slot_sums(rows, router, groups):
    count, depth = rows.shape
    slots = router.shape[1]
    width = depth // ZL
    return pl.pallas_call(
        functools.partial(slot_kernel, groups),
        out_shape=(
            jax.ShapeDtypeStruct((slots * ZL, width + EXTRA), BF),
            jax.ShapeDtypeStruct((slots, count), BF),
        ),
        in_specs=[pl.BlockSpec(memory_space=pltpu.HBM), pl.BlockSpec(memory_space=pltpu.HBM)],
        out_specs=(pl.BlockSpec(memory_space=pltpu.VMEM), pl.BlockSpec(memory_space=pltpu.VMEM)),
        scratch_shapes=[
            pltpu.VMEM((count, depth), BF),
            pltpu.VMEM((slots, depth), BF),
            pltpu.SemaphoreType.DMA((2,)),
        ],
        compiler_params=pltpu.CompilerParams(vmem_limit_bytes=32 * 1024 * 1024),
        name="slot_sums",
    )(in_hbm(rows), in_hbm(router.T))


def exact_parts(v):
    high = lax.reduce_precision(v, 8, 7)
    rest = v - high
    mid = lax.reduce_precision(rest, 8, 7)
    low = rest - mid
    return jnp.stack([high, mid, low], axis=-1).astype(BF)


def packed(mean, lse):
    tail = jnp.pad(exact_parts(lse), [(0, 0)] * lse.ndim + [(0, EXTRA - 3)])
    return jnp.concatenate([mean.astype(BF), tail], axis=-1)


def merged(pieces, width):
    mean = pieces[..., :width].astype(F32)
    lse = jnp.sum(pieces[..., width : width + 3].astype(F32), axis=-1)
    top = jnp.max(lse, axis=0)
    weight = jnp.exp(lse - top)
    total = jnp.sum(weight, axis=0)
    mean = jnp.sum(mean * weight[..., None], axis=0) / total[..., None]
    return mean, top + jnp.log(total)


def scatter(pieces, y0):
    count, width = pieces.shape
    order = rolled((Y, y0), (ZL, 0), (X, X0), (C, 0))
    pieces = pieces.reshape(count, 2, width // 2)
    got = lax.all_to_all(pieces, NEAR, 0, 0, tiled=True, axis_index_groups=order)
    return got.reshape(Y * ZL, count // (Y * ZL), width)


def spread(block, axes, order):
    copies = jnp.broadcast_to(block[None], (len(order[0]),) + block.shape)
    return lax.all_to_all(copies, axes, 0, 0, tiled=True, axis_index_groups=order)


def on_device(patches, router, w_in, w_out):
    own = w_in.shape[0]
    slots = router.shape[1]
    groups = slots // own
    depth = patches.shape[2]
    width = depth // ZL

    pieces, combine = slot_sums(patches[0], router, groups)
    mean, lse = merged(scatter(pieces, Y0), width)
    got = spread(packed(mean, lse), "zh", rolled((ZH, H0)))
    mean, _ = merged(got, width)
    got = spread(mean.astype(BF), ("y", "zl"), rolled((Y, 0), (ZL, 0)))
    slot_in = got.reshape(Y, ZL, groups, width).transpose(2, 0, 1, 3).reshape(groups, own, depth)

    hidden = jax.nn.gelu(jnp.einsum("bed,edf->bef", slot_in, w_in, preferred_element_type=F32)).astype(BF)
    partial_out = jnp.einsum("bef,efd->bed", hidden, w_out, preferred_element_type=F32).astype(BF)

    pieces = partial_out.reshape(groups, Y, ZL, width).transpose(1, 2, 0, 3).reshape(Y * ZL * groups, width)
    total = jnp.sum(scatter(pieces, 0).astype(F32), axis=0).astype(BF)
    got = spread(total, "zh", rolled((ZH, H0)))
    total = jnp.sum(got.astype(F32), axis=0).astype(BF)
    got = spread(total, ("y", "zl"), rolled((Y, Y0), (ZL, 0)))
    slot_out = got.reshape(Y, ZL, groups, width).transpose(0, 2, 1, 3).reshape(slots, depth)

    mixed = lax.dot_general(combine, slot_out, (((0,), (0,)), ((), ())), preferred_element_type=F32)
    return mixed.astype(BF)[None]


def solution(mesh):
    fine = Mesh(mesh.devices.reshape(Y, ZH, ZL, X, C), ("y", "zh", "zl", "x", "c"))
    ctx, exp = ("y", "zh", "zl"), ("x", "c")
    placed = (P(exp, ctx, None), P(), P(exp, None, ctx), P(exp, ctx, None))
    return jax.shard_map(
        on_device, mesh=fine, in_specs=placed, out_specs=P(exp, ctx, None), check_vma=False
    )
```

```python
import functools

import jax
import jax.numpy as jnp
from jax import lax
from jax.experimental import pallas as pl
from jax.experimental.pallas import tpu as pltpu
from jax.sharding import Mesh, PartitionSpec as P

Y, Z, X, C = 4, 16, 4, 2
ZL = 2
ZH = Z // ZL
EXTRA = 128
BF = jnp.bfloat16
F32 = jnp.float32
NEAR = ("y", "zl", "x", "c")
Y0, X0, H0 = 2, 2, ZH // 2


def rolled(*dims):
    members = [0]
    for size, first in dims:
        members = [m * size + (first + i) % size for m in members for i in range(size)]
    return [members]


def slot_kernel(groups, rows_hbm, router_hbm, pieces_ref, combine_ref, rows, router_in, sems):
    count, depth = rows_hbm.shape
    width = depth // ZL
    first = pltpu.make_async_copy(router_hbm, router_in, sems.at[0])
    second = pltpu.make_async_copy(rows_hbm, rows, sems.at[1])
    first.start()
    second.start()
    first.wait()

    slots = router_in.shape[0]
    row = lax.broadcasted_iota(jnp.int32, (slots, slots), 0)
    column = lax.broadcasted_iota(jnp.int32, (slots, slots), 1)
    chosen = (column == ((row + X0 * C) % groups) * Y + row // groups).astype(F32).astype(BF)
    router = jnp.dot(chosen, router_in[...], preferred_element_type=F32).astype(BF)
    second.wait()
    values = lax.dot_general(router, rows[...], (((1,), (1,)), ((), ())), preferred_element_type=F32)
    top = jnp.max(values, axis=1, keepdims=True)
    weights = jnp.exp(values - top)
    total = jnp.sum(weights, axis=1, keepdims=True)
    summed = jnp.dot(weights.astype(BF), rows[...], preferred_element_type=F32)
    mean = summed / total
    lse = top + jnp.log(total)
    high = lse.astype(BF).astype(F32)
    mid = (lse - high).astype(BF).astype(F32)
    low = lse - high - mid
    lane = lax.broadcasted_iota(jnp.int32, (slots, EXTRA), 1)
    tail = jnp.where(lane == 0, high, jnp.where(lane == 1, mid, jnp.where(lane == 2, low, 0.0)))
    size = groups * ZL
    for y in range(Y):
        block = mean[y * groups : (y + 1) * groups]
        halves = [block[:, z * width : (z + 1) * width] for z in range(ZL)]
        pieces_ref[y * size : (y + 1) * size, :width] = jnp.concatenate(halves, axis=0).astype(BF)
        end = tail[y * groups : (y + 1) * groups]
        pieces_ref[y * size : (y + 1) * size, width:] = jnp.concatenate([end] * ZL, axis=0).astype(BF)

    combine = jnp.exp(values - jnp.max(values, axis=0, keepdims=True))
    combine_ref[...] = (combine / jnp.sum(combine, axis=0, keepdims=True)).astype(BF)


def in_hbm(array):
    return pltpu.with_memory_space_constraint(array, pltpu.HBM)


def slot_sums(rows, router, groups):
    count, depth = rows.shape
    slots = router.shape[1]
    width = depth // ZL
    return pl.pallas_call(
        functools.partial(slot_kernel, groups),
        out_shape=(
            jax.ShapeDtypeStruct((slots * ZL, width + EXTRA), BF),
            jax.ShapeDtypeStruct((slots, count), BF),
        ),
        in_specs=[pl.BlockSpec(memory_space=pltpu.HBM), pl.BlockSpec(memory_space=pltpu.HBM)],
        out_specs=(pl.BlockSpec(memory_space=pltpu.VMEM), pl.BlockSpec(memory_space=pltpu.VMEM)),
        scratch_shapes=[
            pltpu.VMEM((count, depth), BF),
            pltpu.VMEM((slots, depth), BF),
            pltpu.SemaphoreType.DMA((2,)),
        ],
        compiler_params=pltpu.CompilerParams(vmem_limit_bytes=32 * 1024 * 1024),
        name="slot_sums",
    )(in_hbm(rows), in_hbm(router.T))


def exact_parts(v):
    high = lax.reduce_precision(v, 8, 7)
    rest = v - high
    mid = lax.reduce_precision(rest, 8, 7)
    low = rest - mid
    return jnp.stack([high, mid, low], axis=-1).astype(BF)


def packed(mean, lse):
    tail = jnp.pad(exact_parts(lse), [(0, 0)] * lse.ndim + [(0, EXTRA - 3)])
    return jnp.concatenate([mean.astype(BF), tail], axis=-1)


def merged(pieces, width):
    mean = pieces[..., :width].astype(F32)
    lse = jnp.sum(pieces[..., width : width + 3].astype(F32), axis=-1)
    top = jnp.max(lse, axis=0)
    weight = jnp.exp(lse - top)
    total = jnp.sum(weight, axis=0)
    mean = jnp.sum(mean * weight[..., None], axis=0) / total[..., None]
    return mean, top + jnp.log(total)


def scatter(pieces):
    count, width = pieces.shape
    order = rolled((Y, Y0), (ZL, 0), (X, X0), (C, 0))
    pieces = pieces.reshape(count, 2, width // 2)
    got = lax.all_to_all(pieces, NEAR, 0, 0, tiled=True, axis_index_groups=order)
    return got.reshape(Y * ZL, count // (Y * ZL), width)


def spread(block, axes, order):
    copies = jnp.broadcast_to(block[None], (len(order[0]),) + block.shape)
    return lax.all_to_all(copies, axes, 0, 0, tiled=True, axis_index_groups=order)


def on_device(patches, router, w_in, w_out):
    own = w_in.shape[0]
    slots = router.shape[1]
    groups = slots // own
    depth = patches.shape[2]
    width = depth // ZL

    pieces, combine = slot_sums(patches[0], router, groups)
    mean, lse = merged(scatter(pieces), width)
    got = spread(packed(mean, lse), "zh", rolled((ZH, H0)))
    mean, _ = merged(got, width)
    got = spread(mean.astype(BF), ("y", "zl"), rolled((Y, Y0), (ZL, 0)))
    slot_in = got.reshape(Y, ZL, groups, width).transpose(2, 0, 1, 3).reshape(groups, own, depth)

    hidden = jax.nn.gelu(jnp.einsum("bed,edf->bef", slot_in, w_in, preferred_element_type=F32)).astype(BF)
    partial_out = jnp.einsum("bef,efd->bed", hidden, w_out, preferred_element_type=F32).astype(BF)

    pieces = partial_out.reshape(groups, Y, ZL, width).transpose(1, 2, 0, 3).reshape(Y * ZL * groups, width)
    total = jnp.sum(scatter(pieces).astype(F32), axis=0).astype(BF)
    got = spread(total, "zh", rolled((ZH, H0)))
    total = jnp.sum(got.astype(F32), axis=0).astype(BF)
    got = spread(total, ("y", "zl"), rolled((Y, Y0), (ZL, 0)))
    slot_out = got.reshape(Y, ZL, groups, width).transpose(0, 2, 1, 3).reshape(slots, depth)

    mixed = lax.dot_general(combine, slot_out, (((0,), (0,)), ((), ())), preferred_element_type=F32)
    return mixed.astype(BF)[None]


def solution(mesh):
    fine = Mesh(mesh.devices.reshape(Y, ZH, ZL, X, C), ("y", "zh", "zl", "x", "c"))
    ctx, exp = ("y", "zh", "zl"), ("x", "c")
    placed = (P(exp, ctx, None), P(), P(exp, None, ctx), P(exp, ctx, None))
    return jax.shard_map(
        on_device, mesh=fine, in_specs=placed, out_specs=P(exp, ctx, None), check_vma=False
    )
```

```python
import functools

import jax
import jax.numpy as jnp
from jax import lax
from jax.experimental import pallas as pl
from jax.experimental.pallas import tpu as pltpu
from jax.sharding import Mesh, PartitionSpec as P

Y, Z, X, C = 4, 16, 4, 2
ZL = 2
ZH = Z // ZL
EXTRA = 128
BF = jnp.bfloat16
F32 = jnp.float32
NEAR = ("y", "zl", "x", "c")
Y0, X0, H0 = 3, 3, 5


def rolled(*dims):
    members = [0]
    for size, first in dims:
        members = [m * size + (first + i) % size for m in members for i in range(size)]
    return [members]


def slot_kernel(groups, rows_hbm, router_hbm, pieces_ref, combine_ref, rows, router_in, sems):
    count, depth = rows_hbm.shape
    width = depth // ZL
    first = pltpu.make_async_copy(router_hbm, router_in, sems.at[0])
    second = pltpu.make_async_copy(rows_hbm, rows, sems.at[1])
    first.start()
    second.start()
    first.wait()

    slots = router_in.shape[0]
    row = lax.broadcasted_iota(jnp.int32, (slots, slots), 0)
    column = lax.broadcasted_iota(jnp.int32, (slots, slots), 1)
    chosen = (column == ((row + X0 * C) % groups) * Y + row // groups).astype(F32).astype(BF)
    router = jnp.dot(chosen, router_in[...], preferred_element_type=F32).astype(BF)
    second.wait()
    values = lax.dot_general(router, rows[...], (((1,), (1,)), ((), ())), preferred_element_type=F32)
    top = jnp.max(values, axis=1, keepdims=True)
    weights = jnp.exp(values - top)
    total = jnp.sum(weights, axis=1, keepdims=True)
    summed = jnp.dot(weights.astype(BF), rows[...], preferred_element_type=F32)
    mean = summed / total
    lse = top + jnp.log(total)
    high = lse.astype(BF).astype(F32)
    mid = (lse - high).astype(BF).astype(F32)
    low = lse - high - mid
    lane = lax.broadcasted_iota(jnp.int32, (slots, EXTRA), 1)
    tail = jnp.where(lane == 0, high, jnp.where(lane == 1, mid, jnp.where(lane == 2, low, 0.0)))
    size = groups * ZL
    for y in range(Y):
        block = mean[y * groups : (y + 1) * groups]
        halves = [block[:, z * width : (z + 1) * width] for z in range(ZL)]
        pieces_ref[y * size : (y + 1) * size, :width] = jnp.concatenate(halves, axis=0).astype(BF)
        end = tail[y * groups : (y + 1) * groups]
        pieces_ref[y * size : (y + 1) * size, width:] = jnp.concatenate([end] * ZL, axis=0).astype(BF)

    combine = jnp.exp(values - jnp.max(values, axis=0, keepdims=True))
    combine_ref[...] = (combine / jnp.sum(combine, axis=0, keepdims=True)).astype(BF)


def in_hbm(array):
    return pltpu.with_memory_space_constraint(array, pltpu.HBM)


def slot_sums(rows, router, groups):
    count, depth = rows.shape
    slots = router.shape[1]
    width = depth // ZL
    return pl.pallas_call(
        functools.partial(slot_kernel, groups),
        out_shape=(
            jax.ShapeDtypeStruct((slots * ZL, width + EXTRA), BF),
            jax.ShapeDtypeStruct((slots, count), BF),
        ),
        in_specs=[pl.BlockSpec(memory_space=pltpu.HBM), pl.BlockSpec(memory_space=pltpu.HBM)],
        out_specs=(pl.BlockSpec(memory_space=pltpu.VMEM), pl.BlockSpec(memory_space=pltpu.VMEM)),
        scratch_shapes=[
            pltpu.VMEM((count, depth), BF),
            pltpu.VMEM((slots, depth), BF),
            pltpu.SemaphoreType.DMA((2,)),
        ],
        compiler_params=pltpu.CompilerParams(vmem_limit_bytes=32 * 1024 * 1024),
        name="slot_sums",
    )(in_hbm(rows), in_hbm(router.T))


def exact_parts(v):
    high = lax.reduce_precision(v, 8, 7)
    rest = v - high
    mid = lax.reduce_precision(rest, 8, 7)
    low = rest - mid
    return jnp.stack([high, mid, low], axis=-1).astype(BF)


def packed(mean, lse):
    tail = jnp.pad(exact_parts(lse), [(0, 0)] * lse.ndim + [(0, EXTRA - 3)])
    return jnp.concatenate([mean.astype(BF), tail], axis=-1)


def merged(pieces, width):
    mean = pieces[..., :width].astype(F32)
    lse = jnp.sum(pieces[..., width : width + 3].astype(F32), axis=-1)
    top = jnp.max(lse, axis=0)
    weight = jnp.exp(lse - top)
    total = jnp.sum(weight, axis=0)
    mean = jnp.sum(mean * weight[..., None], axis=0) / total[..., None]
    return mean, top + jnp.log(total)


def scatter(pieces):
    count, width = pieces.shape
    order = rolled((Y, Y0), (ZL, 0), (X, X0), (C, 0))
    pieces = pieces.reshape(count, 2, width // 2)
    got = lax.all_to_all(pieces, NEAR, 0, 0, tiled=True, axis_index_groups=order)
    return got.reshape(Y * ZL, count // (Y * ZL), width)


def spread(block, axes, order):
    copies = jnp.broadcast_to(block[None], (len(order[0]),) + block.shape)
    return lax.all_to_all(copies, axes, 0, 0, tiled=True, axis_index_groups=order)


def on_device(patches, router, w_in, w_out):
    own = w_in.shape[0]
    slots = router.shape[1]
    groups = slots // own
    depth = patches.shape[2]
    width = depth // ZL

    pieces, combine = slot_sums(patches[0], router, groups)
    mean, lse = merged(scatter(pieces), width)
    got = spread(packed(mean, lse), "zh", rolled((ZH, H0)))
    mean, _ = merged(got, width)
    got = spread(mean.astype(BF), ("y", "zl"), rolled((Y, Y0), (ZL, 0)))
    slot_in = got.reshape(Y, ZL, groups, width).transpose(2, 0, 1, 3).reshape(groups, own, depth)

    hidden = jax.nn.gelu(jnp.einsum("bed,edf->bef", slot_in, w_in, preferred_element_type=F32)).astype(BF)
    partial_out = jnp.einsum("bef,efd->bed", hidden, w_out, preferred_element_type=F32).astype(BF)

    pieces = partial_out.reshape(groups, Y, ZL, width).transpose(1, 2, 0, 3).reshape(Y * ZL * groups, width)
    total = jnp.sum(scatter(pieces).astype(F32), axis=0).astype(BF)
    got = spread(total, "zh", rolled((ZH, H0)))
    total = jnp.sum(got.astype(F32), axis=0).astype(BF)
    got = spread(total, ("y", "zl"), rolled((Y, Y0), (ZL, 0)))
    slot_out = got.reshape(Y, ZL, groups, width).transpose(0, 2, 1, 3).reshape(slots, depth)

    mixed = lax.dot_general(combine, slot_out, (((0,), (0,)), ((), ())), preferred_element_type=F32)
    return mixed.astype(BF)[None]


def solution(mesh):
    fine = Mesh(mesh.devices.reshape(Y, ZH, ZL, X, C), ("y", "zh", "zl", "x", "c"))
    ctx, exp = ("y", "zh", "zl"), ("x", "c")
    placed = (P(exp, ctx, None), P(), P(exp, None, ctx), P(exp, ctx, None))
    return jax.shard_map(
        on_device, mesh=fine, in_specs=placed, out_specs=P(exp, ctx, None), check_vma=False
    )
```

```python
import functools

import jax
import jax.numpy as jnp
from jax import lax
from jax.experimental import pallas as pl
from jax.experimental.pallas import tpu as pltpu
from jax.sharding import Mesh, PartitionSpec as P

Y, Z, X, C = 4, 16, 4, 2
ZL = 2
ZH = Z // ZL
EXTRA = 128
BF = jnp.bfloat16
F32 = jnp.float32
NEAR = ("y", "zl", "x", "c")
Y0, X0 = 3, 3
LONG_IN, LONG_OUT = [[5, 4, 6, 3, 7, 2, 0, 1]], [[5, 0, 1, 2, 7, 3, 6, 4]]


def rolled(*dims):
    members = [0]
    for size, first in dims:
        members = [m * size + (first + i) % size for m in members for i in range(size)]
    return [members]


def slot_kernel(groups, rows_hbm, router_hbm, pieces_ref, combine_ref, rows, router_in, sems):
    count, depth = rows_hbm.shape
    width = depth // ZL
    first = pltpu.make_async_copy(router_hbm, router_in, sems.at[0])
    second = pltpu.make_async_copy(rows_hbm, rows, sems.at[1])
    first.start()
    second.start()
    first.wait()

    slots = router_in.shape[0]
    row = lax.broadcasted_iota(jnp.int32, (slots, slots), 0)
    column = lax.broadcasted_iota(jnp.int32, (slots, slots), 1)
    chosen = (column == ((row + X0 * C) % groups) * Y + row // groups).astype(F32).astype(BF)
    router = jnp.dot(chosen, router_in[...], preferred_element_type=F32).astype(BF)
    second.wait()
    values = lax.dot_general(router, rows[...], (((1,), (1,)), ((), ())), preferred_element_type=F32)
    top = jnp.max(values, axis=1, keepdims=True)
    weights = jnp.exp(values - top)
    total = jnp.sum(weights, axis=1, keepdims=True)
    summed = jnp.dot(weights.astype(BF), rows[...], preferred_element_type=F32)
    mean = summed / total
    lse = top + jnp.log(total)
    high = lse.astype(BF).astype(F32)
    mid = (lse - high).astype(BF).astype(F32)
    low = lse - high - mid
    lane = lax.broadcasted_iota(jnp.int32, (slots, EXTRA), 1)
    tail = jnp.where(lane == 0, high, jnp.where(lane == 1, mid, jnp.where(lane == 2, low, 0.0)))
    size = groups * ZL
    for y in range(Y):
        block = mean[y * groups : (y + 1) * groups]
        halves = [block[:, z * width : (z + 1) * width] for z in range(ZL)]
        pieces_ref[y * size : (y + 1) * size, :width] = jnp.concatenate(halves, axis=0).astype(BF)
        end = tail[y * groups : (y + 1) * groups]
        pieces_ref[y * size : (y + 1) * size, width:] = jnp.concatenate([end] * ZL, axis=0).astype(BF)

    combine = jnp.exp(values - jnp.max(values, axis=0, keepdims=True))
    combine_ref[...] = (combine / jnp.sum(combine, axis=0, keepdims=True)).astype(BF)


def in_hbm(array):
    return pltpu.with_memory_space_constraint(array, pltpu.HBM)


def slot_sums(rows, router, groups):
    count, depth = rows.shape
    slots = router.shape[1]
    width = depth // ZL
    return pl.pallas_call(
        functools.partial(slot_kernel, groups),
        out_shape=(
            jax.ShapeDtypeStruct((slots * ZL, width + EXTRA), BF),
            jax.ShapeDtypeStruct((slots, count), BF),
        ),
        in_specs=[pl.BlockSpec(memory_space=pltpu.HBM), pl.BlockSpec(memory_space=pltpu.HBM)],
        out_specs=(pl.BlockSpec(memory_space=pltpu.VMEM), pl.BlockSpec(memory_space=pltpu.VMEM)),
        scratch_shapes=[
            pltpu.VMEM((count, depth), BF),
            pltpu.VMEM((slots, depth), BF),
            pltpu.SemaphoreType.DMA((2,)),
        ],
        compiler_params=pltpu.CompilerParams(vmem_limit_bytes=32 * 1024 * 1024),
        name="slot_sums",
    )(in_hbm(rows), in_hbm(router.T))


def exact_parts(v):
    high = lax.reduce_precision(v, 8, 7)
    rest = v - high
    mid = lax.reduce_precision(rest, 8, 7)
    low = rest - mid
    return jnp.stack([high, mid, low], axis=-1).astype(BF)


def packed(mean, lse):
    tail = jnp.pad(exact_parts(lse), [(0, 0)] * lse.ndim + [(0, EXTRA - 3)])
    return jnp.concatenate([mean.astype(BF), tail], axis=-1)


def merged(pieces, width):
    mean = pieces[..., :width].astype(F32)
    lse = jnp.sum(pieces[..., width : width + 3].astype(F32), axis=-1)
    top = jnp.max(lse, axis=0)
    weight = jnp.exp(lse - top)
    total = jnp.sum(weight, axis=0)
    mean = jnp.sum(mean * weight[..., None], axis=0) / total[..., None]
    return mean, top + jnp.log(total)


def scatter(pieces):
    count, width = pieces.shape
    order = rolled((Y, Y0), (ZL, 0), (X, X0), (C, 0))
    pieces = pieces.reshape(count, 2, width // 2)
    got = lax.all_to_all(pieces, NEAR, 0, 0, tiled=True, axis_index_groups=order)
    return got.reshape(Y * ZL, count // (Y * ZL), width)


def spread(block, axes, order):
    copies = jnp.broadcast_to(block[None], (len(order[0]),) + block.shape)
    return lax.all_to_all(copies, axes, 0, 0, tiled=True, axis_index_groups=order)


def on_device(patches, router, w_in, w_out):
    own = w_in.shape[0]
    slots = router.shape[1]
    groups = slots // own
    depth = patches.shape[2]
    width = depth // ZL

    pieces, combine = slot_sums(patches[0], router, groups)
    mean, lse = merged(scatter(pieces), width)
    got = spread(packed(mean, lse), "zh", LONG_IN)
    mean, _ = merged(got, width)
    got = spread(mean.astype(BF), ("y", "zl"), rolled((Y, Y0), (ZL, 0)))
    slot_in = got.reshape(Y, ZL, groups, width).transpose(2, 0, 1, 3).reshape(groups, own, depth)

    hidden = jax.nn.gelu(jnp.einsum("bed,edf->bef", slot_in, w_in, preferred_element_type=F32)).astype(BF)
    partial_out = jnp.einsum("bef,efd->bed", hidden, w_out, preferred_element_type=F32).astype(BF)

    pieces = partial_out.reshape(groups, Y, ZL, width).transpose(1, 2, 0, 3).reshape(Y * ZL * groups, width)
    total = jnp.sum(scatter(pieces).astype(F32), axis=0).astype(BF)
    got = spread(total, "zh", LONG_OUT)
    total = jnp.sum(got.astype(F32), axis=0).astype(BF)
    got = spread(total, ("y", "zl"), rolled((Y, Y0), (ZL, 0)))
    slot_out = got.reshape(Y, ZL, groups, width).transpose(0, 2, 1, 3).reshape(slots, depth)

    mixed = lax.dot_general(combine, slot_out, (((0,), (0,)), ((), ())), preferred_element_type=F32)
    return mixed.astype(BF)[None]


def solution(mesh):
    fine = Mesh(mesh.devices.reshape(Y, ZH, ZL, X, C), ("y", "zh", "zl", "x", "c"))
    ctx, exp = ("y", "zh", "zl"), ("x", "c")
    placed = (P(exp, ctx, None), P(), P(exp, None, ctx), P(exp, ctx, None))
    return jax.shard_map(
        on_device, mesh=fine, in_specs=placed, out_specs=P(exp, ctx, None), check_vma=False
    )
```

```python
import functools

import jax
import jax.numpy as jnp
from jax import lax
from jax.experimental import pallas as pl
from jax.experimental.pallas import tpu as pltpu
from jax.sharding import Mesh, PartitionSpec as P

Y, Z, X, C = 4, 16, 4, 2
ZL = 2
ZH = Z // ZL
EXTRA = 128
BF = jnp.bfloat16
F32 = jnp.float32
NEAR = ("y", "zl", "x", "c")
Y0, X0, C0, H0 = 3, 3, 1, 5
ROWS = 128


def rolled(*dims):
    members = [0]
    for size, first in dims:
        members = [m * size + (first + i) % size for m in members for i in range(size)]
    return [members]


def slot_kernel(groups, rows_hbm, router_hbm, pieces_ref, combine_ref, rows, router_in, sems):
    count, depth = rows_hbm.shape
    width = depth // ZL
    first = pltpu.make_async_copy(router_hbm, router_in, sems.at[0])
    second = pltpu.make_async_copy(rows_hbm, rows, sems.at[1])
    first.start()
    second.start()
    first.wait()

    slots = router_in.shape[0]
    row = lax.broadcasted_iota(jnp.int32, (slots, slots), 0)
    column = lax.broadcasted_iota(jnp.int32, (slots, slots), 1)
    owner = (row + X0 * C) % groups // C * C + (row + C0) % C
    chosen = (column == owner * Y + row // groups).astype(F32).astype(BF)
    router = jnp.dot(chosen, router_in[...], preferred_element_type=F32).astype(BF)
    second.wait()
    values = lax.dot_general(router, rows[...], (((1,), (1,)), ((), ())), preferred_element_type=F32)
    top = jnp.max(values, axis=1, keepdims=True)
    weights = jnp.exp(values - top)
    total = jnp.sum(weights, axis=1, keepdims=True)
    summed = jnp.dot(weights.astype(BF), rows[...], preferred_element_type=F32)
    mean = summed / total
    lse = top + jnp.log(total)
    high = lse.astype(BF).astype(F32)
    mid = (lse - high).astype(BF).astype(F32)
    low = lse - high - mid
    lane = lax.broadcasted_iota(jnp.int32, (slots, EXTRA), 1)
    tail = jnp.where(lane == 0, high, jnp.where(lane == 1, mid, jnp.where(lane == 2, low, 0.0)))
    size = groups * ZL
    for y in range(Y):
        block = mean[y * groups : (y + 1) * groups]
        halves = [block[:, z * width : (z + 1) * width] for z in range(ZL)]
        pieces_ref[y * size : (y + 1) * size, :width] = jnp.concatenate(halves, axis=0).astype(BF)
        end = tail[y * groups : (y + 1) * groups]
        pieces_ref[y * size : (y + 1) * size, width:] = jnp.concatenate([end] * ZL, axis=0).astype(BF)

    combine = jnp.exp(values - jnp.max(values, axis=0, keepdims=True))
    combine_ref[...] = (combine / jnp.sum(combine, axis=0, keepdims=True)).astype(BF)


def in_hbm(array):
    return pltpu.with_memory_space_constraint(array, pltpu.HBM)


def slot_sums(rows, router, groups):
    count, depth = rows.shape
    slots = router.shape[1]
    width = depth // ZL
    return pl.pallas_call(
        functools.partial(slot_kernel, groups),
        out_shape=(
            jax.ShapeDtypeStruct((slots * ZL, width + EXTRA), BF),
            jax.ShapeDtypeStruct((slots, count), BF),
        ),
        in_specs=[pl.BlockSpec(memory_space=pltpu.HBM), pl.BlockSpec(memory_space=pltpu.HBM)],
        out_specs=(pl.BlockSpec(memory_space=pltpu.VMEM), pl.BlockSpec(memory_space=pltpu.VMEM)),
        scratch_shapes=[
            pltpu.VMEM((count, depth), BF),
            pltpu.VMEM((slots, depth), BF),
            pltpu.SemaphoreType.DMA((2,)),
        ],
        compiler_params=pltpu.CompilerParams(vmem_limit_bytes=32 * 1024 * 1024),
        name="slot_sums",
    )(in_hbm(rows), in_hbm(router.T))


def mix_kernel(combine_ref, slots_ref, mixed_hbm, mixed, sems):
    copies = []
    for i in range(mixed.shape[0] // ROWS):
        part = pl.ds(i * ROWS, ROWS)
        mixed[part] = lax.dot_general(
            combine_ref[:, part], slots_ref[...], (((0,), (0,)), ((), ())), preferred_element_type=F32
        ).astype(BF)
        copies.append(pltpu.make_async_copy(mixed.at[part], mixed_hbm.at[part], sems.at[i]))
        copies[-1].start()
    for copy in copies:
        copy.wait()


def mix(combine, slot_out):
    count, depth = combine.shape[1], slot_out.shape[1]
    return pl.pallas_call(
        mix_kernel,
        out_shape=jax.ShapeDtypeStruct((count, depth), BF),
        in_specs=[pl.BlockSpec(memory_space=pltpu.VMEM), pl.BlockSpec(memory_space=pltpu.VMEM)],
        out_specs=pl.BlockSpec(memory_space=pl.ANY),
        scratch_shapes=[pltpu.VMEM((count, depth), BF), pltpu.SemaphoreType.DMA((count // ROWS,))],
        compiler_params=pltpu.CompilerParams(vmem_limit_bytes=32 * 1024 * 1024),
        name="mix",
    )(combine, slot_out)


def exact_parts(v):
    high = lax.reduce_precision(v, 8, 7)
    rest = v - high
    mid = lax.reduce_precision(rest, 8, 7)
    low = rest - mid
    return jnp.stack([high, mid, low], axis=-1).astype(BF)


def packed(mean, lse):
    tail = jnp.pad(exact_parts(lse), [(0, 0)] * lse.ndim + [(0, EXTRA - 3)])
    return jnp.concatenate([mean.astype(BF), tail], axis=-1)


def merged(pieces, width):
    mean = pieces[..., :width].astype(F32)
    lse = jnp.sum(pieces[..., width : width + 3].astype(F32), axis=-1)
    top = jnp.max(lse, axis=0)
    weight = jnp.exp(lse - top)
    total = jnp.sum(weight, axis=0)
    mean = jnp.sum(mean * weight[..., None], axis=0) / total[..., None]
    return mean, top + jnp.log(total)


def scatter(pieces):
    count, width = pieces.shape
    order = rolled((Y, Y0), (ZL, 0), (X, X0), (C, C0))
    pieces = pieces.reshape(count, 2, width // 2)
    got = lax.all_to_all(pieces, NEAR, 0, 0, tiled=True, axis_index_groups=order)
    return got.reshape(Y * ZL, count // (Y * ZL), width)


def spread(block, axes, order):
    copies = jnp.broadcast_to(block[None], (len(order[0]),) + block.shape)
    return lax.all_to_all(copies, axes, 0, 0, tiled=True, axis_index_groups=order)


def on_device(patches, router, w_in, w_out):
    own = w_in.shape[0]
    slots = router.shape[1]
    groups = slots // own
    depth = patches.shape[2]
    width = depth // ZL

    pieces, combine = slot_sums(patches[0], router, groups)
    mean, lse = merged(scatter(pieces), width)
    got = spread(packed(mean, lse), "zh", rolled((ZH, H0)))
    mean, _ = merged(got, width)
    got = spread(mean.astype(BF), ("y", "zl"), rolled((Y, Y0), (ZL, 0)))
    slot_in = got.reshape(Y, ZL, groups, width).transpose(2, 0, 1, 3).reshape(groups, own, depth)

    hidden = jax.nn.gelu(jnp.einsum("bed,edf->bef", slot_in, w_in, preferred_element_type=F32)).astype(BF)
    partial_out = jnp.einsum("bef,efd->bed", hidden, w_out, preferred_element_type=F32).astype(BF)

    pieces = partial_out.reshape(groups, Y, ZL, width).transpose(1, 2, 0, 3).reshape(Y * ZL * groups, width)
    total = jnp.sum(scatter(pieces).astype(F32), axis=0).astype(BF)
    got = spread(total, "zh", rolled((ZH, H0)))
    total = jnp.sum(got.astype(F32), axis=0).astype(BF)
    got = spread(total, ("y", "zl"), rolled((Y, Y0), (ZL, 0)))
    slot_out = got.reshape(Y, ZL, groups, width).transpose(0, 2, 1, 3).reshape(slots, depth)

    return mix(combine, slot_out)[None]


def solution(mesh):
    fine = Mesh(mesh.devices.reshape(Y, ZH, ZL, X, C), ("y", "zh", "zl", "x", "c"))
    ctx, exp = ("y", "zh", "zl"), ("x", "c")
    placed = (P(exp, ctx, None), P(), P(exp, None, ctx), P(exp, ctx, None))
    return jax.shard_map(
        on_device, mesh=fine, in_specs=placed, out_specs=P(exp, ctx, None), check_vma=False
    )
```

```python
import functools

import jax
import jax.numpy as jnp
from jax import lax
from jax.experimental import pallas as pl
from jax.experimental.pallas import tpu as pltpu
from jax.sharding import Mesh, PartitionSpec as P

Y, Z, X, C = 4, 16, 4, 2
ZL = 2
EXTRA = 128
ROWS = 128
BF = jnp.bfloat16
F32 = jnp.float32
AXES = ("y", "z", "x", "c")
Y0, X0, C0 = 3, 3, 1
HALVES = ((0, 2, 4, 6, 9, 11, 13, 15), (1, 3, 5, 7, 8, 10, 12, 14))
LONG_IN, LONG_OUT = (11, 10), (9, 10)


def member(y, z, x, c):
    return ((y % Y * Z + z) * X + x % X) * C + c % C


def near_groups():
    return [
        [
            member(Y0 + y, half[k], X0 + x, C0 + c)
            for y in range(Y)
            for half in HALVES
            for x in range(X)
            for c in range(C)
        ]
        for k in range(Z // ZL)
    ]


def gather_groups():
    return [
        [member(Y0 + y, half[k], x, c) for y in range(Y) for half in HALVES]
        for k in range(Z // ZL)
        for x in range(X)
        for c in range(C)
    ]


def long_groups(starts):
    groups = []
    for half, start in zip(HALVES, starts):
        first = half.index(start)
        planes = half[first:] + half[:first]
        groups += [[member(y, z, x, c) for z in planes] for y in range(Y) for x in range(X) for c in range(C)]
    return groups


def slot_kernel(groups, rows_hbm, router_hbm, pieces_ref, combine_ref, rows, router_in, sems):
    count, depth = rows_hbm.shape
    width = depth // ZL
    first = pltpu.make_async_copy(router_hbm, router_in, sems.at[0])
    second = pltpu.make_async_copy(rows_hbm, rows, sems.at[1])
    first.start()
    second.start()
    first.wait()

    slots = router_in.shape[0]
    row = lax.broadcasted_iota(jnp.int32, (slots, slots), 0)
    column = lax.broadcasted_iota(jnp.int32, (slots, slots), 1)
    owner = (row + X0 * C) % groups // C * C + (row + C0) % C
    chosen = (column == owner * Y + row // groups).astype(F32).astype(BF)
    router = jnp.dot(chosen, router_in[...], preferred_element_type=F32).astype(BF)
    second.wait()
    values = lax.dot_general(router, rows[...], (((1,), (1,)), ((), ())), preferred_element_type=F32)
    top = jnp.max(values, axis=1, keepdims=True)
    weights = jnp.exp(values - top)
    total = jnp.sum(weights, axis=1, keepdims=True)
    summed = jnp.dot(weights.astype(BF), rows[...], preferred_element_type=F32)
    mean = summed / total
    lse = top + jnp.log(total)
    high = lse.astype(BF).astype(F32)
    mid = (lse - high).astype(BF).astype(F32)
    low = lse - high - mid
    lane = lax.broadcasted_iota(jnp.int32, (slots, EXTRA), 1)
    tail = jnp.where(lane == 0, high, jnp.where(lane == 1, mid, jnp.where(lane == 2, low, 0.0)))
    size = groups * ZL
    for y in range(Y):
        block = mean[y * groups : (y + 1) * groups]
        halves = [block[:, z * width : (z + 1) * width] for z in range(ZL)]
        pieces_ref[y * size : (y + 1) * size, :width] = jnp.concatenate(halves, axis=0).astype(BF)
        end = tail[y * groups : (y + 1) * groups]
        pieces_ref[y * size : (y + 1) * size, width:] = jnp.concatenate([end] * ZL, axis=0).astype(BF)

    combine = jnp.exp(values - jnp.max(values, axis=0, keepdims=True))
    combine_ref[...] = (combine / jnp.sum(combine, axis=0, keepdims=True)).astype(BF)


def in_hbm(array):
    return pltpu.with_memory_space_constraint(array, pltpu.HBM)


def slot_sums(rows, router, groups):
    count, depth = rows.shape
    slots = router.shape[1]
    width = depth // ZL
    return pl.pallas_call(
        functools.partial(slot_kernel, groups),
        out_shape=(
            jax.ShapeDtypeStruct((slots * ZL, width + EXTRA), BF),
            jax.ShapeDtypeStruct((slots, count), BF),
        ),
        in_specs=[pl.BlockSpec(memory_space=pltpu.HBM), pl.BlockSpec(memory_space=pltpu.HBM)],
        out_specs=(pl.BlockSpec(memory_space=pltpu.VMEM), pl.BlockSpec(memory_space=pltpu.VMEM)),
        scratch_shapes=[
            pltpu.VMEM((count, depth), BF),
            pltpu.VMEM((slots, depth), BF),
            pltpu.SemaphoreType.DMA((2,)),
        ],
        compiler_params=pltpu.CompilerParams(vmem_limit_bytes=32 * 1024 * 1024),
        name="slot_sums",
    )(in_hbm(rows), in_hbm(router.T))


def mix_kernel(combine_ref, slots_ref, mixed_hbm, mixed, sems):
    copies = []
    for i in range(mixed.shape[0] // ROWS):
        part = pl.ds(i * ROWS, ROWS)
        mixed[part] = lax.dot_general(
            combine_ref[:, part], slots_ref[...], (((0,), (0,)), ((), ())), preferred_element_type=F32
        ).astype(BF)
        copies.append(pltpu.make_async_copy(mixed.at[part], mixed_hbm.at[part], sems.at[i]))
        copies[-1].start()
    for copy in copies:
        copy.wait()


def mix(combine, slot_out):
    count, depth = combine.shape[1], slot_out.shape[1]
    return pl.pallas_call(
        mix_kernel,
        out_shape=jax.ShapeDtypeStruct((count, depth), BF),
        in_specs=[pl.BlockSpec(memory_space=pltpu.VMEM), pl.BlockSpec(memory_space=pltpu.VMEM)],
        out_specs=pl.BlockSpec(memory_space=pl.ANY),
        scratch_shapes=[pltpu.VMEM((count, depth), BF), pltpu.SemaphoreType.DMA((count // ROWS,))],
        compiler_params=pltpu.CompilerParams(vmem_limit_bytes=32 * 1024 * 1024),
        name="mix",
    )(combine, slot_out)


def exact_parts(v):
    high = lax.reduce_precision(v, 8, 7)
    rest = v - high
    mid = lax.reduce_precision(rest, 8, 7)
    low = rest - mid
    return jnp.stack([high, mid, low], axis=-1).astype(BF)


def packed(mean, lse):
    tail = jnp.pad(exact_parts(lse), [(0, 0)] * lse.ndim + [(0, EXTRA - 3)])
    return jnp.concatenate([mean.astype(BF), tail], axis=-1)


def merged(pieces, width):
    mean = pieces[..., :width].astype(F32)
    lse = jnp.sum(pieces[..., width : width + 3].astype(F32), axis=-1)
    top = jnp.max(lse, axis=0)
    weight = jnp.exp(lse - top)
    total = jnp.sum(weight, axis=0)
    mean = jnp.sum(mean * weight[..., None], axis=0) / total[..., None]
    return mean, top + jnp.log(total)


def exchange(pieces, groups):
    return lax.all_to_all(pieces, AXES, 0, 0, tiled=True, axis_index_groups=groups)


def scatter(pieces):
    count, width = pieces.shape
    got = exchange(pieces.reshape(count, 2, width // 2), near_groups())
    return got.reshape(Y * ZL, count // (Y * ZL), width)


def spread(block, groups):
    return exchange(jnp.broadcast_to(block[None], (len(groups[0]),) + block.shape), groups)


def on_device(patches, router, w_in, w_out):
    own = w_in.shape[0]
    slots = router.shape[1]
    groups = slots // own
    depth = patches.shape[2]
    width = depth // ZL

    pieces, combine = slot_sums(patches[0], router, groups)
    mean, lse = merged(scatter(pieces), width)
    got = spread(packed(mean, lse), long_groups(LONG_IN))
    mean, _ = merged(got, width)
    got = spread(mean.astype(BF), gather_groups())
    slot_in = got.reshape(Y, ZL, groups, width).transpose(2, 0, 1, 3).reshape(groups, own, depth)

    hidden = jax.nn.gelu(jnp.einsum("bed,edf->bef", slot_in, w_in, preferred_element_type=F32)).astype(BF)
    partial_out = jnp.einsum("bef,efd->bed", hidden, w_out, preferred_element_type=F32).astype(BF)

    pieces = partial_out.reshape(groups, Y, ZL, width).transpose(1, 2, 0, 3).reshape(Y * ZL * groups, width)
    total = jnp.sum(scatter(pieces).astype(F32), axis=0).astype(BF)
    got = spread(total, long_groups(LONG_OUT))
    total = jnp.sum(got.astype(F32), axis=0).astype(BF)
    got = spread(total, gather_groups())
    slot_out = got.reshape(Y, ZL, groups, width).transpose(0, 2, 1, 3).reshape(slots, depth)

    return mix(combine, slot_out)[None]


def solution(mesh):
    fine = Mesh(mesh.devices.reshape(Y, Z, X, C), AXES)
    ctx, exp = AXES[:2], AXES[2:]
    placed = (P(exp, ctx, None), P(), P(exp, None, ctx), P(exp, ctx, None))
    return jax.shard_map(
        on_device, mesh=fine, in_specs=placed, out_specs=P(exp, ctx, None), check_vma=False
    )
```

```python
import functools

import jax
import jax.numpy as jnp
from jax import lax
from jax.experimental import pallas as pl
from jax.experimental.pallas import tpu as pltpu
from jax.sharding import Mesh, PartitionSpec as P

Y, Z, X, C = 4, 16, 4, 2
ZL = 2
EXTRA = 128
ROWS = 128
BF = jnp.bfloat16
F32 = jnp.float32
AXES = ("y", "z", "x", "c")
Y0, X0, C0 = 3, 3, 1
HALVES = ((0, 2, 4, 6, 9, 11, 13, 15), (1, 3, 5, 7, 8, 10, 12, 14))
LONG_IN, LONG_OUT = (11, 10), (9, 10)


def member(y, z, x, c):
    return ((y % Y * Z + z) * X + x % X) * C + c % C


def near_groups():
    return [
        [
            member(Y0 + y, half[k], X0 + x, C0 + c)
            for y in range(Y)
            for half in HALVES
            for x in range(X)
            for c in range(C)
        ]
        for k in range(Z // ZL)
    ]


def gather_groups():
    return [
        [member(Y0 + y, half[k], x, c) for y in range(Y) for half in HALVES]
        for k in range(Z // ZL)
        for x in range(X)
        for c in range(C)
    ]


def long_groups(starts):
    groups = []
    for half, start in zip(HALVES, starts):
        first = half.index(start)
        planes = half[first:] + half[:first]
        groups += [[member(y, z, x, c) for z in planes] for y in range(Y) for x in range(X) for c in range(C)]
    return groups


def slot_kernel(groups, rows_hbm, router_hbm, pieces_ref, combine_ref, rows, router_in, sems):
    count, depth = rows_hbm.shape
    width = depth // ZL
    first = pltpu.make_async_copy(router_hbm, router_in, sems.at[0])
    second = pltpu.make_async_copy(rows_hbm, rows, sems.at[1])
    first.start()
    second.start()
    first.wait()

    slots = router_in.shape[0]
    row = lax.broadcasted_iota(jnp.int32, (slots, slots), 0)
    column = lax.broadcasted_iota(jnp.int32, (slots, slots), 1)
    owner = (row + X0 * C) % groups // C * C + (row + C0) % C
    chosen = (column == owner * Y + row // groups).astype(F32).astype(BF)
    router = jnp.dot(chosen, router_in[...], preferred_element_type=F32).astype(BF)
    second.wait()
    values = lax.dot_general(router, rows[...], (((1,), (1,)), ((), ())), preferred_element_type=F32)
    top = jnp.max(values, axis=1, keepdims=True)
    weights = jnp.exp(values - top)
    total = jnp.sum(weights, axis=1, keepdims=True)
    summed = jnp.dot(weights.astype(BF), rows[...], preferred_element_type=F32)
    mean = summed / total
    lse = top + jnp.log(total)
    high = lse.astype(BF).astype(F32)
    mid = (lse - high).astype(BF).astype(F32)
    low = lse - high - mid
    lane = lax.broadcasted_iota(jnp.int32, (slots, EXTRA), 1)
    tail = jnp.where(lane == 0, high, jnp.where(lane == 1, mid, jnp.where(lane == 2, low, 0.0)))
    size = groups * ZL
    for y in range(Y):
        block = mean[y * groups : (y + 1) * groups]
        halves = [block[:, z * width : (z + 1) * width] for z in range(ZL)]
        pieces_ref[y * size : (y + 1) * size, :width] = jnp.concatenate(halves, axis=0).astype(BF)
        end = tail[y * groups : (y + 1) * groups]
        pieces_ref[y * size : (y + 1) * size, width:] = jnp.concatenate([end] * ZL, axis=0).astype(BF)

    combine = jnp.exp(values - jnp.max(values, axis=0, keepdims=True))
    combine_ref[...] = (combine / jnp.sum(combine, axis=0, keepdims=True)).astype(BF)


def in_hbm(array):
    return pltpu.with_memory_space_constraint(array, pltpu.HBM)


def slot_sums(rows, router, groups):
    count, depth = rows.shape
    slots = router.shape[1]
    width = depth // ZL
    return pl.pallas_call(
        functools.partial(slot_kernel, groups),
        out_shape=(
            jax.ShapeDtypeStruct((slots * ZL, width + EXTRA), BF),
            jax.ShapeDtypeStruct((slots, count), BF),
        ),
        in_specs=[pl.BlockSpec(memory_space=pltpu.HBM), pl.BlockSpec(memory_space=pltpu.HBM)],
        out_specs=(pl.BlockSpec(memory_space=pltpu.VMEM), pl.BlockSpec(memory_space=pltpu.VMEM)),
        scratch_shapes=[
            pltpu.VMEM((count, depth), BF),
            pltpu.VMEM((slots, depth), BF),
            pltpu.SemaphoreType.DMA((2,)),
        ],
        compiler_params=pltpu.CompilerParams(vmem_limit_bytes=32 * 1024 * 1024),
        name="slot_sums",
    )(in_hbm(rows), in_hbm(router.T))


def mix_kernel(combine_ref, slots_ref, mixed_hbm, mixed, sems):
    copies = []
    for i in range(mixed.shape[0] // ROWS):
        part = pl.ds(i * ROWS, ROWS)
        mixed[part] = lax.dot_general(
            combine_ref[:, part], slots_ref[...], (((0,), (0,)), ((), ())), preferred_element_type=F32
        ).astype(BF)
        copies.append(pltpu.make_async_copy(mixed.at[part], mixed_hbm.at[part], sems.at[i]))
        copies[-1].start()
    for copy in copies:
        copy.wait()


def mix(combine, slot_out):
    count, depth = combine.shape[1], slot_out.shape[1]
    return pl.pallas_call(
        mix_kernel,
        out_shape=jax.ShapeDtypeStruct((count, depth), BF),
        in_specs=[pl.BlockSpec(memory_space=pltpu.VMEM), pl.BlockSpec(memory_space=pltpu.VMEM)],
        out_specs=pl.BlockSpec(memory_space=pl.ANY),
        scratch_shapes=[pltpu.VMEM((count, depth), BF), pltpu.SemaphoreType.DMA((count // ROWS,))],
        compiler_params=pltpu.CompilerParams(vmem_limit_bytes=32 * 1024 * 1024),
        name="mix",
    )(combine, slot_out)


def exact_parts(v):
    high = lax.reduce_precision(v, 8, 7)
    rest = v - high
    mid = lax.reduce_precision(rest, 8, 7)
    low = rest - mid
    return jnp.stack([high, mid, low], axis=-1).astype(BF)


def packed(mean, lse):
    tail = jnp.pad(exact_parts(lse), [(0, 0)] * lse.ndim + [(0, EXTRA - 3)])
    return jnp.concatenate([mean.astype(BF), tail], axis=-1)


def merged(pieces, width):
    mean = pieces[..., :width].astype(F32)
    lse = jnp.sum(pieces[..., width:].astype(F32), axis=-1)
    top = jnp.max(lse, axis=0)
    weight = jnp.exp(lse - top)
    total = jnp.sum(weight, axis=0)
    mean = jnp.sum(mean * weight[..., None], axis=0) / total[..., None]
    return mean, top + jnp.log(total)


def exchange(pieces, groups):
    return lax.all_to_all(pieces, AXES, 0, 0, tiled=True, axis_index_groups=groups)


def scatter(pieces):
    count, width = pieces.shape
    got = exchange(pieces.reshape(count, 2, width // 2), near_groups())
    return got.reshape(Y * ZL, count // (Y * ZL), width)


def spread(block, groups):
    return exchange(jnp.broadcast_to(block[None], (len(groups[0]),) + block.shape), groups)


def on_device(patches, router, w_in, w_out):
    own = w_in.shape[0]
    slots = router.shape[1]
    groups = slots // own
    depth = patches.shape[2]
    width = depth // ZL

    pieces, combine = slot_sums(patches[0], router, groups)
    mean, lse = merged(scatter(pieces), width)
    got = spread(packed(mean, lse), long_groups(LONG_IN))
    mean, _ = merged(got, width)
    got = spread(mean.astype(BF), gather_groups())
    slot_in = got.reshape(Y, ZL, groups, width).transpose(2, 0, 1, 3).reshape(groups, own, depth)

    hidden = jax.nn.gelu(jnp.einsum("bed,edf->bef", slot_in, w_in, preferred_element_type=F32)).astype(BF)
    partial_out = jnp.einsum("bef,efd->bed", hidden, w_out, preferred_element_type=F32).astype(BF)

    pieces = partial_out.reshape(groups, Y, ZL, width).transpose(1, 2, 0, 3).reshape(Y * ZL * groups, width)
    total = jnp.sum(scatter(pieces).astype(F32), axis=0).astype(BF)
    got = spread(total, long_groups(LONG_OUT))
    total = jnp.sum(got.astype(F32), axis=0).astype(BF)
    got = spread(total, gather_groups())
    slot_out = got.reshape(Y, ZL, groups, width).transpose(0, 2, 1, 3).reshape(slots, depth)

    return mix(combine, slot_out)[None]


def solution(mesh):
    fine = Mesh(mesh.devices.reshape(Y, Z, X, C), AXES)
    ctx, exp = AXES[:2], AXES[2:]
    placed = (P(exp, ctx, None), P(), P(exp, None, ctx), P(exp, ctx, None))
    return jax.shard_map(
        on_device, mesh=fine, in_specs=placed, out_specs=P(exp, ctx, None), check_vma=False
    )
```

```python
import functools

import jax
import jax.numpy as jnp
from jax import lax
from jax.experimental import pallas as pl
from jax.experimental.pallas import tpu as pltpu
from jax.sharding import Mesh, PartitionSpec as P

Y, Z, X, C = 4, 16, 4, 2
ZL = 2
EXTRA = 128
ROWS = 128
BF = jnp.bfloat16
F32 = jnp.float32
AXES = ("y", "z", "x", "c")
Y0, X0, C0 = 3, 3, 1
HALVES = ((0, 2, 4, 6, 9, 11, 13, 15), (1, 3, 5, 7, 8, 10, 12, 14))
LONG_IN, LONG_OUT = (11, 10), (9, 10)


def member(y, z, x, c):
    return ((y % Y * Z + z) * X + x % X) * C + c % C


def near_groups():
    return [
        [
            member(Y0 + y, half[k], X0 + x, C0 + c)
            for y in range(Y)
            for half in HALVES
            for x in range(X)
            for c in range(C)
        ]
        for k in range(Z // ZL)
    ]


def gather_groups():
    return [
        [member(Y0 + y, half[k], x, c) for y in range(Y) for half in HALVES]
        for k in range(Z // ZL)
        for x in range(X)
        for c in range(C)
    ]


def long_groups(starts):
    groups = []
    for half, start in zip(HALVES, starts):
        first = half.index(start)
        planes = half[first:] + half[:first]
        groups += [[member(y, z, x, c) for z in planes] for y in range(Y) for x in range(X) for c in range(C)]
    return groups


def slot_kernel(groups, rows_hbm, router_hbm, pieces_ref, combine_ref, rows, router_in, sems):
    count, depth = rows_hbm.shape
    width = depth // ZL
    first = pltpu.make_async_copy(router_hbm, router_in, sems.at[0])
    second = pltpu.make_async_copy(rows_hbm, rows, sems.at[1])
    first.start()
    second.start()
    first.wait()

    slots = router_in.shape[0]
    row = lax.broadcasted_iota(jnp.int32, (slots, slots), 0)
    column = lax.broadcasted_iota(jnp.int32, (slots, slots), 1)
    owner = (row + X0 * C) % groups // C * C + (row + C0) % C
    chosen = (column == owner * Y + row // groups).astype(F32).astype(BF)
    router = jnp.dot(chosen, router_in[...], preferred_element_type=F32).astype(BF)
    second.wait()
    values = lax.dot_general(router, rows[...], (((1,), (1,)), ((), ())), preferred_element_type=F32)
    top = jnp.max(values, axis=1, keepdims=True)
    weights = jnp.exp(values - top)
    total = jnp.sum(weights, axis=1, keepdims=True)
    summed = jnp.dot(weights.astype(BF), rows[...], preferred_element_type=F32)
    mean = summed / total
    lse = top + jnp.log(total)
    high = lse.astype(BF).astype(F32)
    mid = (lse - high).astype(BF).astype(F32)
    low = lse - high - mid
    lane = lax.broadcasted_iota(jnp.int32, (slots, EXTRA), 1)
    tail = jnp.where(lane == 0, high, jnp.where(lane == 1, mid, jnp.where(lane == 2, low, 0.0)))
    size = groups * ZL
    for y in range(Y):
        block = mean[y * groups : (y + 1) * groups]
        halves = [block[:, z * width : (z + 1) * width] for z in range(ZL)]
        pieces_ref[y * size : (y + 1) * size, :width] = jnp.concatenate(halves, axis=0).astype(BF)
        end = tail[y * groups : (y + 1) * groups]
        pieces_ref[y * size : (y + 1) * size, width:] = jnp.concatenate([end] * ZL, axis=0).astype(BF)

    combine = jnp.exp(values - jnp.max(values, axis=0, keepdims=True))
    combine_ref[...] = (combine / jnp.sum(combine, axis=0, keepdims=True)).astype(BF)


def in_hbm(array):
    return pltpu.with_memory_space_constraint(array, pltpu.HBM)


def slot_sums(rows, router, groups):
    count, depth = rows.shape
    slots = router.shape[1]
    width = depth // ZL
    return pl.pallas_call(
        functools.partial(slot_kernel, groups),
        out_shape=(
            jax.ShapeDtypeStruct((slots * ZL, width + EXTRA), BF),
            jax.ShapeDtypeStruct((slots, count), BF),
        ),
        in_specs=[pl.BlockSpec(memory_space=pltpu.HBM), pl.BlockSpec(memory_space=pltpu.HBM)],
        out_specs=(pl.BlockSpec(memory_space=pltpu.VMEM), pl.BlockSpec(memory_space=pltpu.VMEM)),
        scratch_shapes=[
            pltpu.VMEM((count, depth), BF),
            pltpu.VMEM((slots, depth), BF),
            pltpu.SemaphoreType.DMA((2,)),
        ],
        compiler_params=pltpu.CompilerParams(vmem_limit_bytes=32 * 1024 * 1024),
        name="slot_sums",
    )(in_hbm(rows), in_hbm(router.T))


def mix_kernel(combine_ref, slots_ref, mixed_hbm, mixed, sems):
    copies = []
    for i in range(mixed.shape[0] // ROWS):
        part = pl.ds(i * ROWS, ROWS)
        mixed[part] = lax.dot_general(
            combine_ref[:, part], slots_ref[...], (((0,), (0,)), ((), ())), preferred_element_type=F32
        ).astype(BF)
        copies.append(pltpu.make_async_copy(mixed.at[part], mixed_hbm.at[part], sems.at[i]))
        copies[-1].start()
    for copy in copies:
        copy.wait()


def mix(combine, slot_out):
    count, depth = combine.shape[1], slot_out.shape[1]
    return pl.pallas_call(
        mix_kernel,
        out_shape=jax.ShapeDtypeStruct((count, depth), BF),
        in_specs=[pl.BlockSpec(memory_space=pltpu.VMEM), pl.BlockSpec(memory_space=pltpu.VMEM)],
        out_specs=pl.BlockSpec(memory_space=pl.ANY),
        scratch_shapes=[pltpu.VMEM((count, depth), BF), pltpu.SemaphoreType.DMA((count // ROWS,))],
        compiler_params=pltpu.CompilerParams(vmem_limit_bytes=32 * 1024 * 1024),
        name="mix",
    )(combine, slot_out)


def exact_parts(v):
    high = lax.reduce_precision(v, 8, 7)
    rest = v - high
    mid = lax.reduce_precision(rest, 8, 7)
    low = rest - mid
    return jnp.stack([high, mid, low], axis=-1).astype(BF)


def packed(mean, lse):
    tail = jnp.pad(exact_parts(lse), [(0, 0)] * lse.ndim + [(0, EXTRA - 3)])
    return jnp.concatenate([mean.astype(BF), tail], axis=-1)


def merged(pieces, width):
    mean = pieces[..., :width].astype(F32)
    lse = jnp.sum(pieces[..., width : width + 3].astype(F32), axis=-1)
    top = jnp.max(lse, axis=0)
    weight = jnp.exp(lse - top)
    total = jnp.sum(weight, axis=0)
    mean = jnp.sum(mean * weight[..., None], axis=0) / total[..., None]
    return mean, top + jnp.log(total)


def exchange(pieces, groups):
    return lax.all_to_all(pieces, AXES, 0, 0, tiled=True, axis_index_groups=groups)


def scatter(pieces):
    count, width = pieces.shape
    got = exchange(pieces.reshape(count, 2, width // 2), near_groups())
    return got.reshape(Y * ZL, count // (Y * ZL), width)


def spread(block, groups):
    return exchange(jnp.broadcast_to(block[None], (len(groups[0]),) + block.shape), groups)


def on_device(patches, router, w_in, w_out):
    own = w_in.shape[0]
    slots = router.shape[1]
    groups = slots // own
    depth = patches.shape[2]
    width = depth // ZL

    pieces, combine = slot_sums(patches[0], router, groups)
    mean, lse = merged(scatter(pieces), width)
    got = spread(packed(mean, lse), long_groups(LONG_IN))
    mean, _ = merged(got, width)
    got = spread(mean.astype(BF), gather_groups())
    slot_in = got.reshape(Y, ZL, groups, width).transpose(2, 0, 1, 3).reshape(groups, own, depth)

    hidden = jax.nn.gelu(jnp.einsum("bed,edf->bef", slot_in, w_in, preferred_element_type=F32)).astype(BF)
    partial_out = jnp.einsum("bef,efd->bed", hidden, w_out, preferred_element_type=F32).astype(BF)

    pieces = partial_out.reshape(groups, Y, ZL, width).transpose(1, 2, 0, 3).reshape(Y * ZL * groups, width)
    pieces = jnp.pad(pieces, ((0, 0), (0, EXTRA)))
    total = jnp.sum(scatter(pieces)[..., :width].astype(F32), axis=0).astype(BF)
    got = spread(total, long_groups(LONG_OUT))
    total = jnp.sum(got.astype(F32), axis=0).astype(BF)
    got = spread(total, gather_groups())
    slot_out = got.reshape(Y, ZL, groups, width).transpose(0, 2, 1, 3).reshape(slots, depth)

    return mix(combine, slot_out)[None]


def solution(mesh):
    fine = Mesh(mesh.devices.reshape(Y, Z, X, C), AXES)
    ctx, exp = AXES[:2], AXES[2:]
    placed = (P(exp, ctx, None), P(), P(exp, None, ctx), P(exp, ctx, None))
    return jax.shard_map(
        on_device, mesh=fine, in_specs=placed, out_specs=P(exp, ctx, None), check_vma=False
    )
```
